128 devices in a mesh: tile: 64 (over z, x, y), slab: 2 (over core).
Axes of the slice: x: 4, y: 4, z: 4, core: 2. Of those that a mesh axis runs over, the one named last changes fastest.
Arguments:
- gas_state: float32 [4, 256, 16, 256], P(None, 'tile', None, 'slab'), may hold values from -6 to 6
- sound_speed: float32 [256, 16, 256], P('tile', None, 'slab'), may hold values from 0.5 to 2
- velocity: float32 [3, 64, 2, 32768], P(None, 'tile', 'slab'), may hold values from -6 to 6
- drag_rate: float32 [64, 2, 32768], P('tile', 'slab'), may hold values from 0.05 to 0.9
- parcel_mass: float32 [64, 2, 32768], P('tile', 'slab'), may hold values from 0.2 to 5
- cell_offset: float32 [64, 2, 32768], P('tile', 'slab'), may hold values from -0.5 to 0.5
- target_owner: int32 [64, 2, 32768, 1], P('tile', 'slab'), may hold values from 0 to 127; in each aligned block of 32768 rows (0 to 32767, 32768 to 65535, ..., all dimensions but the last counted through in order) at most 384 rows name the same one
- target_cell: int32 [64, 2, 32768], P('tile', 'slab'), may hold values from 0 to 8191
- live_counts: int32 [64, 2], P('tile', 'slab'), may hold values from 10922 to 32768
Outputs:
- gas_next: float32 [4, 256, 16, 256], P(None, 'tile', None, 'slab')
- moved_velocity: float32 [3, 64, 2, 128, 384], P(None, 'tile', 'slab')
The draws below stay inside these ranges and needn't reach their ends.
Inputs may be any that keep to these rules, and one draw needn't show every extreme that they name: `target_owner`: in each owner's 32768 slots, live or not, at most 384 name the same new owner.
All inputs are finite; a program needn't handle non-finite values.
Results may differ from the reference program's by a relative error of at most 0.0003.
Values sent between devices are 32-bit elements; how exact they have to be, the bound alone decides.
No kernel may reach another device: no remote copies, remote signals or barrier semaphores. Data moves between devices by JAX's collectives and lax.ppermute only.
A program may use at most 192 MiB of HBM per device.

```python
import math
import jax
import jax.numpy as jnp
import numpy as np
from jax import lax

CX = 4
CY = 16
CZ = 128
PCAP = 32768
TILES = 64
SLABS = 2
OWNERS = 128
CAPACITY = 384
NX = 256
NZ = 256


def draw_live_counts(key, part):
    key = jax.random.fold_in(key, 11)
    first_key, second_key = jax.random.split(key)
    values = jax.random.randint(first_key, (TILES * SLABS,), PCAP // 3, PCAP + 1)
    picked = jax.random.permutation(second_key, TILES * SLABS)
    values = values.at[picked[0]].set(PCAP).at[picked[1]].set(PCAP // 3)
    return values.reshape(TILES, SLABS).astype(jnp.int32)


def set_ends(entries, rng, low, top_value):
    longest = entries.shape.index(max(entries.shape))
    spots = []
    for shift in (0, 1):
        where = [jax.random.randint(jax.random.fold_in(rng, axis), (), 0, length) for axis, length in enumerate(entries.shape)]
        where[longest] = (where[longest] + shift) % entries.shape[longest]
        spots.append(tuple(where))
    return entries.at[spots[0]].set(low).at[spots[1]].set(top_value)


def shard_levels(key, dims, pieces, smallest, largest):
    def one(axis_at, shards_of):
        heights = jax.random.uniform(jax.random.fold_in(jax.random.fold_in(key, 6), axis_at), (shards_of,), jnp.float32, smallest / len(pieces), largest / len(pieces))
        return jnp.repeat(jnp.exp(heights), dims[axis_at] // shards_of).reshape((-1,) + (1,) * (len(dims) - axis_at - 1))

    gain = one(*pieces[0])
    for cut in pieces[1:]:
        gain = gain * one(*cut)
    return gain


def assign_block(rng, own, number, rows, count, top, bound, lean):
    sequence = jax.random.permutation(rng, count)
    crowded, common = load_shares(count, rows * top, bound, lean, True), load_shares(count, rows * top, bound, lean, False)
    places = jnp.arange(count)

    def named(sizes, turn):
        used = int((sizes > 0).sum())
        fixed = max(1, used // 4)
        passed = fixed + (places - fixed + turn * (used - fixed)) % max(1, count - fixed)
        return jnp.zeros((count,), jnp.int32).at[sequence[jnp.where(places < fixed, places, passed)]].set(jnp.asarray(sizes, jnp.int32))

    sizes = jnp.where(number % 4 == 0, named(crowded, number // 4), named(common, number - number // 4 - 1))
    mixed = jax.random.permutation(jax.random.fold_in(own, 3), count)
    source_of, sink = mixed[0:count // 2 * 2:2], mixed[1:count // 2 * 2:2]
    room = jnp.minimum(sizes[source_of] - 1, bound - sizes[sink]) // 2
    room = jnp.where((source_of == sequence[0]) | (sink == sequence[0]) | (sizes[sink] == 0), 0, jnp.maximum(room, 0))
    passed = jax.random.randint(jax.random.fold_in(own, 4), (count // 2,), 0, 1 << 20) % (room + 1)
    sizes = sizes.at[source_of].add(-passed).at[sink].add(passed)
    members = jnp.searchsorted(jnp.cumsum(sizes), jnp.arange(rows * top), side="right").astype(jnp.int32)
    listing = members.reshape(top, rows).T
    listing = listing[jax.random.permutation(jax.random.fold_in(own, 1), rows)]
    turn = jax.random.randint(jax.random.fold_in(own, 2), (rows, 1), 0, top)
    return jnp.take_along_axis(listing, (jnp.arange(top)[None, :] + turn) % top, axis=1)


def load_shares(amount, total, most, lean, full):
    loads = [(1 << 20) // math.isqrt(standing ** lean) + 1 for standing in range(1, amount + 1)]
    largest = most if full else min(most, max(-(-total // amount), total * loads[0] // sum(loads)))
    least = 1 if total - largest >= amount - 1 else 0
    holding, rest = [largest] + [least] * (amount - 1), total - largest - least * (amount - 1)
    while rest > 0:
        movable = [i for i in range(1, amount) if holding[i] < largest] or [i for i in range(1, amount) if holding[i] < most]
        mass, budget = sum([loads[i] for i in movable]), rest
        for i in movable:
            extra = min(most - holding[i], max(1, budget * loads[i] // mass), rest)
            holding[i] = holding[i] + extra
            rest = rest - extra
    return np.array(holding)


def gaussian(key, extent, scale, reach, cuts=(), kind=jnp.bfloat16):
    factor_of = shard_levels(key, extent, cuts, -0.22, 0.18) if cuts else 1.0
    array = jax.random.normal(key, extent, jnp.float32) * scale * factor_of
    return jnp.minimum(jnp.maximum(array, -reach), reach).astype(kind)


def setup_inputs(seed: int = 0) -> dict:
    splits = jax.random.split(jax.random.key(seed), 10)
    gas_state = gaussian(splits[0], (4, NX, CY, NZ), 1.0, 6.0, ((1, 64), (3, 2)), jnp.float32)
    sound_speed = jnp.clip(jnp.exp(math.log(2.0) - 1.3862944 * jax.random.uniform(splits[1], (NX, CY, NZ), jnp.float32) ** shard_levels(splits[1], (NX, CY, NZ), ((0, 64), (2, 2)), -0.2, 0.2)), 0.5, 2.0)
    velocity = gaussian(splits[2], (3, TILES, SLABS, PCAP), 1.0, 6.0, ((1, 64), (2, 2)), jnp.float32)
    drag_rate = jnp.clip(jnp.exp(math.log(0.9) - 2.8903717 * jax.random.uniform(splits[3], (TILES, SLABS, PCAP), jnp.float32) ** shard_levels(splits[3], (TILES, SLABS, PCAP), ((0, 64), (1, 2)), -0.2, 0.2)), 0.05, 0.9)
    parcel_mass = jnp.clip(jnp.exp(math.log(5.0) - 3.218876 * jax.random.uniform(splits[4], (TILES, SLABS, PCAP), jnp.float32) ** shard_levels(splits[4], (TILES, SLABS, PCAP), ((0, 64), (1, 2)), -0.2, 0.2)), 0.2, 5.0)
    cell_offset = jnp.clip(jax.random.uniform(splits[5], (TILES, SLABS, PCAP), jnp.float32, -0.5, 0.5) * shard_levels(splits[5], (TILES, SLABS, PCAP), ((0, 64), (1, 2)), -0.4, 0.0), -0.5, 0.5)
    target_owner_keys = jax.random.split(jax.random.fold_in(splits[6], 1), TILES * SLABS * PCAP // PCAP)
    target_owner_turns = jax.random.permutation(jax.random.fold_in(splits[6], 3), TILES * SLABS * PCAP // PCAP)
    target_owner = jax.vmap(lambda own, number: assign_block(jax.random.fold_in(splits[6], 2), own, number, PCAP, OWNERS, 1, CAPACITY, 2))(target_owner_keys, target_owner_turns).reshape((TILES, SLABS, PCAP, 1))
    target_cell = set_ends(jax.random.randint(splits[7], (TILES, SLABS, PCAP), 0, CX * CY * CZ), jax.random.fold_in(splits[7], 1), 0, (CX * CY * CZ) - 1).astype(jnp.int32)
    live_counts = draw_live_counts(jax.random.fold_in(splits[9], 71), 0)
    return dict(gas_state=gas_state, sound_speed=sound_speed, velocity=velocity, drag_rate=drag_rate, parcel_mass=parcel_mass, cell_offset=cell_offset, target_owner=target_owner, target_cell=target_cell, live_counts=live_counts)


courant = 0.4


def fourth(extended, dimension, length):
    def window(position):
        return lax.slice_in_dim(extended, position, position + length, axis=dimension)
    return (8.0 * (window(3) - window(1)) - (window(4) - window(0))) / 12.0


def periodic_extend(field, dimension):
    head = lax.slice_in_dim(field, field.shape[dimension] - 2, field.shape[dimension], axis=dimension)
    tail = lax.slice_in_dim(field, 0, 2, axis=dimension)
    return jnp.concatenate([head, field, tail], axis=dimension)


def zero_extend(field, dimension):
    widths = [(0, 0)] * field.ndim
    widths[dimension] = (2, 2)
    return jnp.pad(field, widths)


def ranks_of(destination):
    owner_count = TILES * SLABS
    ordering = jnp.argsort(destination, stable=True)
    tallies = jnp.zeros((owner_count + 1,), jnp.int32).at[destination].add(1)
    firsts = jnp.cumsum(tallies) - tallies
    sorted_owner = destination[ordering]
    placed = jnp.arange(PCAP, dtype=jnp.int32) - firsts[sorted_owner]
    return jnp.zeros((PCAP,), jnp.int32).at[ordering].set(placed)


def reference(gas_state, sound_speed, velocity, drag_rate, parcel_mass, cell_offset, target_owner, target_cell, live_counts):
    owner_count = TILES * SLABS
    alive_mask = jnp.arange(PCAP, dtype=jnp.int32)[None, None, :] < live_counts[:, :, None]
    destination = jnp.where(alive_mask, target_owner[..., 0], owner_count).reshape(owner_count, PCAP)
    ranking = lax.map(ranks_of, destination)
    sources = jnp.arange(owner_count, dtype=jnp.int32)[:, None]
    slot_index = (destination * (owner_count * CAPACITY) + sources * CAPACITY + ranking).reshape(-1)
    payload = jnp.concatenate([
        velocity.reshape(3, -1), drag_rate.reshape(1, -1), parcel_mass.reshape(1, -1),
        cell_offset.reshape(1, -1), target_cell.reshape(1, -1).astype(jnp.float32)], axis=0)
    total_slots = owner_count * owner_count * CAPACITY
    arrived = jnp.zeros((7, total_slots), jnp.float32).at[:, slot_index].set(payload, mode="drop")
    slot_ids = jnp.arange(total_slots, dtype=jnp.int32)
    owner_ids = slot_ids // (owner_count * CAPACITY)
    tile_of = owner_ids // SLABS
    slab_of = owner_ids % SLABS
    cell_ids = arrived[6].astype(jnp.int32)
    column_x = cell_ids // (CY * CZ)
    row_y = (cell_ids // CZ) % CY
    row_z = cell_ids % CZ
    global_x = tile_of * CX + column_x
    global_z = slab_of * CZ + row_z
    flat_cell = (global_x * CY + row_y) * NZ + global_z
    momentum_flat = gas_state[1:4].reshape(3, -1)
    gas_speed = jnp.take(momentum_flat, flat_cell, axis=1)
    speeds = arrived[0:3]
    rates = arrived[3]
    masses = arrived[4]
    shifts = arrived[5]
    occupied = masses > 0.0
    relaxed = jnp.where(occupied[None, :], speeds + rates[None, :] * (gas_speed - speeds), 0.0)
    moved_velocity = relaxed.reshape(3, TILES, SLABS, owner_count, CAPACITY)
    kicked = (masses * rates)[None, :] * (speeds - gas_speed)
    weight_low = 0.5 * (0.5 - shifts) ** 2
    weight_mid = 0.75 - shifts ** 2
    weight_high = 0.5 * (0.5 + shifts) ** 2
    plane_size = CY * NZ
    remainder = row_y * NZ + global_z
    lower_cell = ((global_x - 1) % NX) * plane_size + remainder
    upper_cell = ((global_x + 1) % NX) * plane_size + remainder
    added = jnp.zeros((3, NX * plane_size), jnp.float32)
    added = added.at[:, lower_cell].add(kicked * weight_low[None, :])
    added = added.at[:, flat_cell].add(kicked * weight_mid[None, :])
    added = added.at[:, upper_cell].add(kicked * weight_high[None, :])
    momentum = gas_state[1:4] + added.reshape(3, NX, CY, NZ)
    pressure = sound_speed * gas_state[0]
    density_next = gas_state[0] - courant * (
        fourth(periodic_extend(momentum[0], 0), 0, NX)
        + fourth(periodic_extend(momentum[1], 1), 1, CY)
        + fourth(zero_extend(momentum[2], 2), 2, NZ))
    first_next = momentum[0] - courant * fourth(periodic_extend(pressure, 0), 0, NX)
    second_next = momentum[1] - courant * fourth(periodic_extend(pressure, 1), 1, CY)
    third_next = momentum[2] - courant * fourth(zero_extend(pressure, 2), 2, NZ)
    gas_next = jnp.stack([density_next, first_next, second_next, third_next])
    return gas_next, moved_velocity
```

```python
import jax
import jax.numpy as jnp
from jax import lax
from jax.experimental import pallas as pl
from jax.experimental.pallas import tpu as pltpu
from jax.sharding import PartitionSpec as P

courant = 0.4
LANES = 128
COLUMNS = 256
RES = 64
ROWS = 16
SOURCES = 8
FIELDS = 7
VMEM_BYTES = 40 * 1024 * 1024
NT = (((1,), (1,)), ((), ()))
NN = (((1,), (0,)), ((), ()))


def split2(x):
    hi = x.astype(jnp.bfloat16).astype(jnp.float32)
    return hi, x - hi


def dispatch_kernel(
    live_ref, vel_ref, rate_ref, mass_ref, off_ref, owner_ref, cell_ref, out_ref,
    acc, values, lead, onehot, owners, base, combined,
):
    owner_count = base.shape[0]
    windows = acc.shape[1]
    groups = acc.shape[2]
    pitch = out_ref.shape[0] // owner_count
    chunk = ROWS * LANES
    step = pl.program_id(0)
    f32, bf16 = jnp.float32, jnp.bfloat16

    @pl.when(step == 0)
    def _():
        acc[...] = jnp.zeros_like(acc)
        base[...] = jnp.zeros_like(base)

    slot = (
        step * chunk
        + lax.broadcasted_iota(jnp.int32, (ROWS, LANES), 0) * LANES
        + lax.broadcasted_iota(jnp.int32, (ROWS, LANES), 1)
    )
    alive = slot < live_ref[0, 0]
    dest = jnp.where(alive, owner_ref[...], owner_count)

    owner_row = lax.broadcasted_iota(jnp.int32, (owner_count, LANES), 0)
    for j in range(ROWS):
        owners[:, j * LANES : (j + 1) * LANES] = jnp.where(
            dest[j : j + 1, :] == owner_row, 1.0, 0.0
        ).astype(bf16)
    before = lax.broadcasted_iota(jnp.int32, (COLUMNS, COLUMNS), 0)
    after = lax.broadcasted_iota(jnp.int32, (COLUMNS, COLUMNS), 1)
    upper = jnp.where(before < after, 1.0, 0.0).astype(bf16)
    ones = jnp.full((COLUMNS, LANES), 1.0, bf16)
    start = base[...]
    running = start * float(chunk)
    for t in range(ROWS // 2):
        tile = owners[:, t * COLUMNS : (t + 1) * COLUMNS]
        prior = lax.dot_general(tile, upper, NN, preferred_element_type=f32)
        count = lax.dot_general(tile, ones, NN, preferred_element_type=f32)
        for half in range(2):
            j = 2 * t + half
            total = prior[:, half * LANES : (half + 1) * LANES] + running
            mask = dest[j : j + 1, :] == owner_row
            combined[j : j + 1, :] = jnp.sum(
                jnp.where(mask, total, 0.0), axis=0, keepdims=True
            )
        running = running + count
    tally = running - start * float(chunk)
    base[...] = start + tally
    passes = (jnp.max(tally).astype(jnp.int32) + RES - 1) // RES
    both = combined[...].astype(jnp.int32)
    local_rank = both & (chunk - 1)
    rank = local_rank + both // chunk
    column = (dest // groups) * RES + (rank & (RES - 1))
    turn = jnp.where(alive, local_rank // RES, -1)
    group = dest & (groups - 1)

    fields = [
        vel_ref[0], vel_ref[1], vel_ref[2], rate_ref[...], mass_ref[...], off_ref[...],
        cell_ref[...].astype(f32),
    ]
    group_row = lax.broadcasted_iota(jnp.int32, (groups, LANES), 0)
    width = FIELDS * groups
    for v, field in enumerate(fields):
        hi, lo = split2(field)
        values[v] = hi
        values[v + FIELDS] = lo
    for j in range(ROWS):
        mask = group[j : j + 1, :] == group_row
        for v in range(2 * FIELDS):
            lead[v * groups : (v + 1) * groups, j * LANES : (j + 1) * LANES] = jnp.where(
                mask, values[v, j : j + 1, :], 0.0
            ).astype(bf16)

    column_row = lax.broadcasted_iota(jnp.int32, (COLUMNS, LANES), 0)
    lane = lax.broadcasted_iota(jnp.int32, (groups, LANES), 1)
    starts = start.astype(jnp.int32)

    def one_pass(number, carry):
        picked = jnp.where(turn == number, column, -1)
        for j in range(ROWS):
            onehot[:, j * LANES : (j + 1) * LANES] = jnp.where(
                picked[j : j + 1, :] == column_row, 1.0, 0.0
            ).astype(bf16)
        product = lax.dot_general(lead[...], onehot[...], NT, preferred_element_type=f32)
        product = product[:width] + product[width:]
        for k in range(COLUMNS // LANES):
            cols = slice(k * LANES, (k + 1) * LANES)
            even = starts[2 * k * groups : (2 * k + 1) * groups]
            odd = starts[(2 * k + 1) * groups : (2 * k + 2) * groups]
            first = jnp.where(lane < RES, even, odd) + number * RES
            window = (first + (((lane & (RES - 1)) - first) & (RES - 1))) // RES
            for w in range(windows):
                here = window == w
                for v in range(FIELDS):
                    acc[v, w, :, cols] += jnp.where(
                        here, product[v * groups : (v + 1) * groups, cols], 0.0
                    )
        return carry

    lax.fori_loop(0, passes, one_pass, 0)

    @pl.when(step == pl.num_programs(0) - 1)
    def _():
        low = lax.broadcasted_iota(jnp.int32, (8, LANES), 1) < RES
        for v in range(FIELDS):
            for k in range(COLUMNS // LANES):
                cols = slice(k * LANES, (k + 1) * LANES)
                for m in range(windows // 2):
                    for part in range(groups // 8):
                        rows = slice(part * 8, (part + 1) * 8)
                        one = acc[v, 2 * m, rows, cols]
                        two = acc[v, 2 * m + 1, rows, cols]
                        place = v * (windows // 2) + m
                        even = (2 * k * groups + part * 8) * pitch + place
                        odd = ((2 * k + 1) * groups + part * 8) * pitch + place
                        out_ref[pl.ds(even, 8, stride=pitch), :] = jnp.where(
                            low, one, pltpu.roll(two, RES, 1)
                        )
                        out_ref[pl.ds(odd, 8, stride=pitch), :] = jnp.where(
                            low, pltpu.roll(one, RES, 1), two
                        )


def dispatch(live, vel, rate, mass, off, owner, cell, owner_count, capacity):
    rows = rate.shape[0]
    groups = owner_count * RES // COLUMNS
    chunk = ROWS * LANES
    pitch = FIELDS * capacity // LANES
    plain = pl.BlockSpec((ROWS, LANES), lambda i: (i, 0))
    return pl.pallas_call(
        dispatch_kernel,
        grid=(rows // ROWS,),
        in_specs=[
            pl.BlockSpec(memory_space=pltpu.SMEM),
            pl.BlockSpec((3, ROWS, LANES), lambda i: (0, i, 0)),
            plain, plain, plain, plain, plain,
        ],
        out_specs=pl.BlockSpec((owner_count * pitch, LANES), lambda i: (0, 0)),
        out_shape=jax.ShapeDtypeStruct((owner_count * pitch, LANES), jnp.float32),
        scratch_shapes=[
            pltpu.VMEM((FIELDS, capacity // RES, groups, COLUMNS), jnp.float32),
            pltpu.VMEM((2 * FIELDS, ROWS, LANES), jnp.float32),
            pltpu.VMEM((2 * FIELDS * groups, chunk), jnp.bfloat16),
            pltpu.VMEM((COLUMNS, chunk), jnp.bfloat16),
            pltpu.VMEM((owner_count, chunk), jnp.bfloat16),
            pltpu.VMEM((owner_count, LANES), jnp.float32),
            pltpu.VMEM((ROWS, LANES), jnp.float32),
        ],
        compiler_params=pltpu.CompilerParams(vmem_limit_bytes=VMEM_BYTES),
        name="dispatch",
    )(live, vel, rate, mass, off, owner, cell)


def deposit_kernel(
    arrived_ref, gas_ref, moved_ref, dep_ref, table, total, onehot, lead, speeds, pieces
):
    capacity = moved_ref.shape[2]
    width_x = gas_ref.shape[1]
    reach = width_x + 2
    strips = 8
    rows = width_x * strips
    pitch = arrived_ref.shape[0] // SOURCES
    parts = capacity // LANES
    f32, bf16 = jnp.float32, jnp.bfloat16
    step = pl.program_id(0)

    @pl.when(step == 0)
    def _():
        total[...] = jnp.zeros_like(total)
        for v in range(3):
            for x in range(0, width_x, 2):
                for h in range(2):
                    two = [gas_ref[1 + v, x + i, h * 8 : (h + 1) * 8, :] for i in range(2)]
                    hi, lo = split2(jnp.concatenate(two, axis=0))
                    at = v * rows + x * strips
                    cols = slice(h * LANES, (h + 1) * LANES)
                    table[at : at + 16, cols] = hi.astype(bf16)
                    table[3 * rows + at : 3 * rows + at + 16, cols] = lo.astype(bf16)

    def field(v):
        return jnp.concatenate(
            [arrived_ref[pl.ds(v * parts + m, SOURCES, stride=pitch), :] for m in range(parts)],
            axis=1,
        )

    cell = field(6).astype(jnp.int32)
    column = (cell & (LANES - 1)) + ((cell >> 10) & 1) * LANES
    plane = cell >> 11
    strip = (cell >> 7) & 7
    row = plane * strips + strip
    column_row = lax.broadcasted_iota(jnp.int32, (COLUMNS, capacity), 0)
    for s in range(SOURCES):
        onehot[:, s * capacity : (s + 1) * capacity] = jnp.where(
            column[s : s + 1, :] == column_row, 1.0, 0.0
        ).astype(bf16)
    found = lax.dot_general(table[...], onehot[...], NN, preferred_element_type=f32)
    found = found[: 3 * rows] + found[3 * rows :]
    row_row = lax.broadcasted_iota(jnp.int32, (rows, capacity), 0)
    for s in range(SOURCES):
        mask = row[s : s + 1, :] == row_row
        for v in range(3):
            speeds[v, s : s + 1, :] = jnp.sum(
                jnp.where(
                    mask,
                    found[v * rows : (v + 1) * rows, s * capacity : (s + 1) * capacity],
                    0.0,
                ),
                axis=0,
                keepdims=True,
            )
    rate = field(3)
    mass = field(4)
    shift = field(5)
    occupied = mass > 0.0
    low_weight = 0.5 * (0.5 - shift) ** 2
    mid_weight = 0.75 - shift**2
    high_weight = 0.5 * (0.5 + shift) ** 2
    weights = []
    for x in range(reach):
        weights.append(
            jnp.where(
                plane == x,
                low_weight,
                jnp.where(plane == x - 1, mid_weight, jnp.where(plane == x - 2, high_weight, 0.0)),
            )
        )
    for v in range(3):
        speed = field(v)
        slip = speed - speeds[v]
        moved_ref[v] = jnp.where(occupied, speed - rate * slip, 0.0)
        kick = mass * rate * slip
        for x in range(reach):
            hi, lo = split2(kick * weights[x])
            pieces[v * reach + x] = hi
            pieces[(3 + v) * reach + x] = lo
    strip_row = lax.broadcasted_iota(jnp.int32, (strips, capacity), 0)
    for s in range(SOURCES):
        mask = strip[s : s + 1, :] == strip_row
        for pair in range(3 * reach):
            both = [jnp.where(mask, pieces[2 * pair + i, s : s + 1, :], 0.0) for i in range(2)]
            lead[pair * 16 : (pair + 1) * 16, s * capacity : (s + 1) * capacity] = (
                jnp.concatenate(both, axis=0).astype(bf16)
            )
    half = 3 * reach * strips
    product = lax.dot_general(lead[...], onehot[...], NT, preferred_element_type=f32)
    total[...] = total[...] + (product[:half] + product[half:])

    @pl.when(step == pl.num_programs(0) - 1)
    def _():
        for v in range(3):
            for x in range(reach):
                at = (v * reach + x) * strips
                for h in range(2):
                    dep_ref[v, x, h * 8 : (h + 1) * 8, :] = total[
                        at : at + strips, h * LANES : (h + 1) * LANES
                    ]


def deposit(arrived, gas, count, capacity):
    pitch = arrived.shape[0] // count
    width_x, width_y, width_z = gas.shape[1:]
    reach = width_x + 2
    deposit_rows = 3 * reach * 8
    return pl.pallas_call(
        deposit_kernel,
        grid=(count // SOURCES,),
        in_specs=[
            pl.BlockSpec((SOURCES * pitch, LANES), lambda i: (i, 0)),
            pl.BlockSpec(gas.shape, lambda i: (0, 0, 0, 0)),
        ],
        out_specs=[
            pl.BlockSpec((3, SOURCES, capacity), lambda i: (0, i, 0)),
            pl.BlockSpec((3, reach, width_y, width_z), lambda i: (0, 0, 0, 0)),
        ],
        out_shape=[
            jax.ShapeDtypeStruct((3, count, capacity), jnp.float32),
            jax.ShapeDtypeStruct((3, reach, width_y, width_z), jnp.float32),
        ],
        scratch_shapes=[
            pltpu.VMEM((6 * width_x * 8, COLUMNS), jnp.bfloat16),
            pltpu.VMEM((deposit_rows, COLUMNS), jnp.float32),
            pltpu.VMEM((COLUMNS, SOURCES * capacity), jnp.bfloat16),
            pltpu.VMEM((2 * deposit_rows, SOURCES * capacity), jnp.bfloat16),
            pltpu.VMEM((3, SOURCES, capacity), jnp.float32),
            pltpu.VMEM((6 * reach, SOURCES, capacity), jnp.float32),
        ],
        compiler_params=pltpu.CompilerParams(vmem_limit_bytes=VMEM_BYTES),
        name="deposit",
    )(arrived, gas)


def step_kernel(
    slab_ref, gas_ref, sound_ref, dep_ref, left_ref, right_ref, other_ref,
    left_other_ref, right_other_ref, left_p_ref, right_p_ref, other_p_ref, next_ref,
):
    width_x, width_y, width_z = sound_ref.shape
    slab = slab_ref[0, 0]
    first_slab = slab == 0
    lane = lax.broadcasted_iota(jnp.int32, (width_y, width_z), 1)

    def along_y(f, shift):
        return pltpu.roll(f, (-shift) % width_y, 0)

    def along_z(f, other, shift):
        turned = pltpu.roll(f, (-shift) % width_z, 1)
        beyond = pltpu.roll(other, (-shift) % width_z, 1)
        if shift > 0:
            inside = lane < width_z - shift
            reached = first_slab
        else:
            inside = lane >= -shift
            reached = jnp.logical_not(first_slab)
        return jnp.where(inside, turned, jnp.where(reached, beyond, 0.0))

    def fourth(shifted):
        return (8.0 * (shifted(1) - shifted(-1)) - (shifted(2) - shifted(-2))) / 12.0

    def momentum(k, x):
        value = gas_ref[1 + k, x] + dep_ref[k, x + 1]
        if x == 0:
            value = value + left_ref[2 + k]
        if x == width_x - 1:
            value = value + right_ref[2 + k]
        return value

    planes = [[momentum(k, x) for x in range(width_x)] for k in range(3)]
    first = {x: planes[0][x] for x in range(width_x)}
    first[-2] = left_ref[0]
    first[-1] = left_ref[1] + dep_ref[0, 0]
    first[width_x] = right_ref[0] + dep_ref[0, width_x + 1]
    first[width_x + 1] = right_ref[1]
    pressure = {x: sound_ref[x] * gas_ref[0, x] for x in range(width_x)}
    pressure[-2] = left_p_ref[0]
    pressure[-1] = left_p_ref[1]
    pressure[width_x] = right_p_ref[0]
    pressure[width_x + 1] = right_p_ref[1]
    for x in range(width_x):
        other = other_ref[x]
        if x == 0:
            other = other + left_other_ref[...]
        if x == width_x - 1:
            other = other + right_other_ref[...]
        other_p = other_p_ref[x]
        p = pressure[x]
        next_ref[0, x] = gas_ref[0, x] - courant * (
            fourth(lambda s: first[x + s])
            + fourth(lambda s: along_y(planes[1][x], s))
            + fourth(lambda s: along_z(planes[2][x], other, s))
        )
        next_ref[1, x] = planes[0][x] - courant * fourth(lambda s: pressure[x + s])
        next_ref[2, x] = planes[1][x] - courant * fourth(lambda s: along_y(p, s))
        next_ref[3, x] = planes[2][x] - courant * fourth(lambda s: along_z(p, other_p, s))


def gas_step(slab, gas, *rest):
    whole = pl.BlockSpec(memory_space=pltpu.VMEM)
    return pl.pallas_call(
        step_kernel,
        in_specs=[pl.BlockSpec(memory_space=pltpu.SMEM)] + [whole] * (1 + len(rest)),
        out_specs=whole,
        out_shape=jax.ShapeDtypeStruct(gas.shape, jnp.float32),
        compiler_params=pltpu.CompilerParams(vmem_limit_bytes=VMEM_BYTES),
        name="gas_step",
    )(slab, gas, *rest)


def per_device(
    gas_state, sound_speed, velocity, drag_rate, parcel_mass, cell_offset, target_owner,
    target_cell, live_counts,
):
    tiles = lax.axis_size("tile")
    slabs = lax.axis_size("slab")
    owner_count = tiles * slabs
    slot_count = target_cell.shape[-1]
    capacity = 3 * slot_count // (2 * owner_count)
    width_x = gas_state.shape[1]
    rows = slot_count // LANES
    to_right = [(t, (t + 1) % tiles) for t in range(tiles)]
    to_left = [(t, (t - 1) % tiles) for t in range(tiles)]
    swap = [(s, slabs - 1 - s) for s in range(slabs)]

    def diagonal(pairs):
        return [(a * slabs + s, b * slabs + r) for a, b in pairs for s, r in swap]

    pressure = sound_speed * gas_state[0]
    left_p = lax.ppermute(pressure[width_x - 2 :], "tile", to_right)
    right_p = lax.ppermute(pressure[:2], "tile", to_left)
    other_p = lax.ppermute(pressure, "slab", swap)

    outbox = dispatch(
        live_counts,
        velocity.reshape(3, rows, LANES),
        drag_rate.reshape(rows, LANES),
        parcel_mass.reshape(rows, LANES),
        cell_offset.reshape(rows, LANES),
        target_owner.reshape(rows, LANES),
        target_cell.reshape(rows, LANES),
        owner_count,
        capacity,
    )
    arrived = lax.all_to_all(
        outbox.reshape(owner_count, 1, FIELDS * capacity), ("tile", "slab"),
        split_axis=0, concat_axis=0, tiled=True,
    ).reshape(outbox.shape)
    moved, dep = deposit(arrived, gas_state, owner_count, capacity)

    first = gas_state[1] + dep[0, 1 : width_x + 1]
    left = lax.ppermute(
        jnp.concatenate([first[width_x - 2 :], dep[:, width_x + 1]]), "tile", to_right
    )
    right = lax.ppermute(jnp.concatenate([first[:2], dep[:, 0]]), "tile", to_left)
    other = lax.ppermute(gas_state[3] + dep[2, 1 : width_x + 1], "slab", swap)
    left_other = lax.ppermute(dep[2, width_x + 1], ("tile", "slab"), diagonal(to_right))
    right_other = lax.ppermute(dep[2, 0], ("tile", "slab"), diagonal(to_left))
    slab = lax.axis_index("slab").astype(jnp.int32).reshape(1, 1)
    gas_next = gas_step(
        slab, gas_state, sound_speed, dep, left, right, other, left_other, right_other,
        left_p, right_p, other_p,
    )
    return gas_next, moved.reshape(3, 1, 1, owner_count, capacity)


def solution(mesh):
    return jax.shard_map(
        per_device,
        mesh=mesh,
        in_specs=(
            P(None, "tile", None, "slab"),
            P("tile", None, "slab"),
            P(None, "tile", "slab", None),
            P("tile", "slab", None),
            P("tile", "slab", None),
            P("tile", "slab", None),
            P("tile", "slab", None, None),
            P("tile", "slab", None),
            P("tile", "slab"),
        ),
        out_specs=(P(None, "tile", None, "slab"), P(None, "tile", "slab", None, None)),
        check_vma=False,
    )
```

```python
import jax
import jax.numpy as jnp
from jax import lax
from jax.experimental import pallas as pl
from jax.experimental.pallas import tpu as pltpu
from jax.sharding import PartitionSpec as P

courant = 0.4
LANES = 128
COLUMNS = 256
RES = 64
ROWS = 16
SOURCES = 8
FIELDS = 7
VMEM_BYTES = 40 * 1024 * 1024
NT = (((1,), (1,)), ((), ()))
NN = (((1,), (0,)), ((), ()))


def split2(x):
    hi = x.astype(jnp.bfloat16).astype(jnp.float32)
    return hi, x - hi


def dispatch_kernel(
    live_ref, vel_ref, rate_ref, mass_ref, off_ref, owner_ref, cell_ref, out_ref,
    acc, values, lead0, lead1, onehot0, onehot1, spare, owners, base, pending, combined,
):
    owner_count = base.shape[0]
    windows = acc.shape[1]
    groups = acc.shape[2]
    pitch = out_ref.shape[0] // owner_count
    chunk = ROWS * LANES
    width = FIELDS * groups
    step = pl.program_id(0)
    f32, bf16 = jnp.float32, jnp.bfloat16
    leads = (lead0, lead1)
    onehots = (onehot0, onehot1)

    @pl.when(step == 0)
    def _():
        acc[...] = jnp.zeros_like(acc)
        base[...] = jnp.zeros_like(base)
        pending[...] = jnp.full_like(pending, -65536.0)

    def short_iota(rows):
        return lax.broadcasted_iota(jnp.int32, (rows, LANES), 0).astype(f32).astype(bf16)

    def short_rows(row):
        return jnp.broadcast_to(row, (16, LANES)).astype(bf16)

    one = jnp.ones((16, LANES), bf16)
    zero = jnp.zeros((16, LANES), bf16)

    def spread(target, row, cols, rows):
        same = short_rows(row)
        numbers = short_iota(rows)
        for b in range(rows // 16):
            block = slice(b * 16, (b + 1) * 16)
            target[block, cols] = jnp.where(same == numbers[block], one, zero)

    def write_onehot(target, picked):
        for j in range(ROWS):
            spread(target, picked[j : j + 1, :], slice(j * LANES, (j + 1) * LANES), COLUMNS)

    def add_product(lead, onehot, start, number):
        product = lax.dot_general(lead[...], onehot[...], NT, preferred_element_type=f32)
        product = product[:width] + product[width:]
        starts = start.astype(jnp.int32)
        lane = lax.broadcasted_iota(jnp.int32, (groups, LANES), 1)
        for k in range(COLUMNS // LANES):
            cols = slice(k * LANES, (k + 1) * LANES)
            even = starts[2 * k * groups : (2 * k + 1) * groups]
            odd = starts[(2 * k + 1) * groups : (2 * k + 2) * groups]
            first = jnp.where(lane < RES, even, odd) + number * RES
            window = (first + (((lane & (RES - 1)) - first) & (RES - 1))) >> 6
            for w in range(windows):
                here = window == w
                for v in range(FIELDS):
                    acc[v, w, :, cols] += jnp.where(
                        here, product[v * groups : (v + 1) * groups, cols], 0.0
                    )

    def build(h):
        part = slice(h * ROWS, (h + 1) * ROWS)
        lead, onehot = leads[h], onehots[h]
        slot = (
            (2 * step + h) * chunk
            + lax.broadcasted_iota(jnp.int32, (ROWS, LANES), 0) * LANES
            + lax.broadcasted_iota(jnp.int32, (ROWS, LANES), 1)
        )
        alive = slot < live_ref[0, 0]
        dest = jnp.where(alive, owner_ref[part], owner_count)
        destf = dest.astype(f32)

        for j in range(ROWS):
            t, half = j // 2, j % 2
            spread(
                owners.at[t * owner_count : (t + 1) * owner_count],
                destf[j : j + 1, :], slice(half * LANES, (half + 1) * LANES), owner_count,
            )
        before = lax.broadcasted_iota(jnp.int32, (COLUMNS, COLUMNS + LANES), 0)
        after = lax.broadcasted_iota(jnp.int32, (COLUMNS, COLUMNS + LANES), 1)
        upper = jnp.where(before < after, 1.0, 0.0).astype(bf16)
        prior = lax.dot_general(owners[...], upper, NN, preferred_element_type=f32)
        owner_row = lax.broadcasted_iota(jnp.int32, (owner_count, LANES), 0)
        start = base[...]
        running = start * float(chunk)
        for t in range(ROWS // 2):
            rows = slice(t * owner_count, (t + 1) * owner_count)
            for half in range(2):
                j = 2 * t + half
                total = prior[rows, half * LANES : (half + 1) * LANES] + running
                combined[j : j + 1, :] = jnp.sum(
                    jnp.where(dest[j : j + 1, :] == owner_row, total, 0.0), axis=0, keepdims=True
                )
            running = running + prior[rows, COLUMNS:]
        tally = running - start * float(chunk)
        base[...] = start + tally
        pending[h] = start
        both = combined[...].astype(jnp.int32)
        local_rank = both & (chunk - 1)
        rank = local_rank + (both >> 11)
        column = (dest // groups) * RES + (rank & (RES - 1))
        turn = jnp.where(alive, local_rank >> 6, -1)

        fields = [
            vel_ref[0, part], vel_ref[1, part], vel_ref[2, part], rate_ref[part], mass_ref[part],
            off_ref[part], cell_ref[part].astype(f32),
        ]
        for v, field in enumerate(fields):
            hi, lo = split2(field)
            values[v] = hi
            values[v + FIELDS] = lo
        group = (dest & (groups - 1)).astype(f32)
        numbers = short_iota(groups)
        for j in range(ROWS):
            same = short_rows(group[j : j + 1, :])
            masks = [same == numbers[b * 16 : (b + 1) * 16] for b in range(groups // 16)]
            for v in range(2 * FIELDS):
                value = short_rows(values[v, j : j + 1, :])
                for b, mask in enumerate(masks):
                    at = v * groups + b * 16
                    lead[at : at + 16, j * LANES : (j + 1) * LANES] = jnp.where(mask, value, zero)
        write_onehot(onehot, jnp.where(turn == 0, column, -1).astype(f32))
        passes = (jnp.max(tally).astype(jnp.int32) + RES - 1) >> 6
        return passes, turn, column, start

    def further(h, state):
        passes, turn, column, start = state

        @pl.when(passes > 1)
        def _():
            def one_pass(number, carry):
                write_onehot(spare, jnp.where(turn == number, column, -1).astype(f32))
                add_product(leads[h], spare, start, number)
                return carry

            lax.fori_loop(1, passes, one_pass, 0)

    late = pending[1]
    states = [build(0)]
    add_product(lead1, onehot1, late, 0)
    states.append(build(1))
    add_product(lead0, onehot0, pending[0], 0)
    for h in range(2):
        further(h, states[h])

    @pl.when(step == pl.num_programs(0) - 1)
    def _():
        add_product(lead1, onehot1, pending[1], 0)
        low = lax.broadcasted_iota(jnp.int32, (8, LANES), 1) < RES
        for v in range(FIELDS):
            for k in range(COLUMNS // LANES):
                cols = slice(k * LANES, (k + 1) * LANES)
                for m in range(windows // 2):
                    for part in range(groups // 8):
                        rows = slice(part * 8, (part + 1) * 8)
                        near = acc[v, 2 * m, rows, cols]
                        far = acc[v, 2 * m + 1, rows, cols]
                        place = v * (windows // 2) + m
                        even = (2 * k * groups + part * 8) * pitch + place
                        odd = ((2 * k + 1) * groups + part * 8) * pitch + place
                        out_ref[pl.ds(even, 8, stride=pitch), :] = jnp.where(
                            low, near, pltpu.roll(far, RES, 1)
                        )
                        out_ref[pl.ds(odd, 8, stride=pitch), :] = jnp.where(
                            low, pltpu.roll(near, RES, 1), far
                        )


def dispatch(live, vel, rate, mass, off, owner, cell, owner_count, capacity):
    rows = rate.shape[0]
    groups = owner_count * RES // COLUMNS
    chunk = ROWS * LANES
    pitch = FIELDS * capacity // LANES
    plain = pl.BlockSpec((2 * ROWS, LANES), lambda i: (i, 0))
    lead = pltpu.VMEM((2 * FIELDS * groups, chunk), jnp.bfloat16)
    onehot = pltpu.VMEM((COLUMNS, chunk), jnp.bfloat16)
    return pl.pallas_call(
        dispatch_kernel,
        grid=(rows // (2 * ROWS),),
        in_specs=[
            pl.BlockSpec(memory_space=pltpu.SMEM),
            pl.BlockSpec((3, 2 * ROWS, LANES), lambda i: (0, i, 0)),
            plain, plain, plain, plain, plain,
        ],
        out_specs=pl.BlockSpec((owner_count * pitch, LANES), lambda i: (0, 0)),
        out_shape=jax.ShapeDtypeStruct((owner_count * pitch, LANES), jnp.float32),
        scratch_shapes=[
            pltpu.VMEM((FIELDS, capacity // RES, groups, COLUMNS), jnp.float32),
            pltpu.VMEM((2 * FIELDS, ROWS, LANES), jnp.float32),
            lead, lead, onehot, onehot, onehot,
            pltpu.VMEM((ROWS // 2 * owner_count, COLUMNS), jnp.bfloat16),
            pltpu.VMEM((owner_count, LANES), jnp.float32),
            pltpu.VMEM((2, owner_count, LANES), jnp.float32),
            pltpu.VMEM((ROWS, LANES), jnp.float32),
        ],
        compiler_params=pltpu.CompilerParams(vmem_limit_bytes=60 * 1024 * 1024),
        name="dispatch",
    )(live, vel, rate, mass, off, owner, cell)


def deposit_kernel(
    arrived_ref, gas_ref, sound_ref,
    moved_ref, raw_ref, to_right_ref, to_left_ref, to_other_ref,
    table, total, onehot0, onehot1, lead0, lead1, speeds, pieces,
):
    capacity = moved_ref.shape[2]
    width_x = gas_ref.shape[1]
    reach = width_x + 2
    strips = 8
    rows = width_x * strips
    half = 3 * reach * strips
    pitch = arrived_ref.shape[0] // (2 * SOURCES)
    parts = capacity // LANES
    f32, bf16 = jnp.float32, jnp.bfloat16
    step = pl.program_id(0)
    leads = (lead0, lead1)
    onehots = (onehot0, onehot1)

    @pl.when(step == 0)
    def _():
        total[...] = jnp.zeros_like(total)
        for v in range(3):
            for x in range(0, width_x, 2):
                for h in range(2):
                    two = [gas_ref[1 + v, x + i, h * 8 : (h + 1) * 8, :] for i in range(2)]
                    hi, lo = split2(jnp.concatenate(two, axis=0))
                    at = v * rows + x * strips
                    cols = slice(h * LANES, (h + 1) * LANES)
                    table[at : at + 16, cols] = hi.astype(bf16)
                    table[3 * rows + at : 3 * rows + at + 16, cols] = lo.astype(bf16)

    one = jnp.ones((16, capacity), bf16)
    zero = jnp.zeros((16, capacity), bf16)
    number = lax.broadcasted_iota(jnp.int32, (16, capacity), 0)
    numbers = [(number + 16 * b).astype(f32).astype(bf16) for b in range(COLUMNS // 16)]
    strip_number = (number & (strips - 1)).astype(f32).astype(bf16)
    row_row = lax.broadcasted_iota(jnp.int32, (rows, capacity), 0)

    def short_rows(row):
        return jnp.broadcast_to(row, (16, capacity)).astype(bf16)

    def spans(s):
        return slice(s * capacity, (s + 1) * capacity)

    def field(h, v):
        first = h * SOURCES * pitch + v * parts
        return jnp.concatenate(
            [arrived_ref[pl.ds(first + m, SOURCES, stride=pitch), :] for m in range(parts)], axis=1
        )

    def look_up(h):
        cell = field(h, 6).astype(jnp.int32)
        column = ((cell & (LANES - 1)) + ((cell >> 10) & 1) * LANES).astype(f32)
        for s in range(SOURCES):
            same = short_rows(column[s : s + 1, :])
            for b in range(COLUMNS // 16):
                onehots[h][b * 16 : (b + 1) * 16, spans(s)] = jnp.where(
                    same == numbers[b], one, zero
                )
        found = lax.dot_general(table[...], onehots[h][...], NN, preferred_element_type=f32)
        return cell, found[: 3 * rows] + found[3 * rows :]

    def relax(h, cell, found):
        part = slice(h * SOURCES, (h + 1) * SOURCES)
        plane = cell >> 11
        strip = (cell >> 7) & (strips - 1)
        row = plane * strips + strip
        for s in range(SOURCES):
            mask = row[s : s + 1, :] == row_row
            for v in range(3):
                speeds[v, s : s + 1, :] = jnp.sum(
                    jnp.where(mask, found[v * rows : (v + 1) * rows, spans(s)], 0.0),
                    axis=0, keepdims=True,
                )
        rate = field(h, 3)
        mass = field(h, 4)
        shift = field(h, 5)
        occupied = mass > 0.0
        low_weight = 0.5 * (0.5 - shift) ** 2
        mid_weight = 0.75 - shift**2
        high_weight = 0.5 * (0.5 + shift) ** 2
        weights = []
        for x in range(reach):
            rest = jnp.where(plane == x - 2, high_weight, 0.0)
            rest = jnp.where(plane == x - 1, mid_weight, rest)
            weights.append(jnp.where(plane == x, low_weight, rest))
        for v in range(3):
            speed = field(h, v)
            slip = speed - speeds[v]
            moved_ref[v, part] = jnp.where(occupied, speed - rate * slip, 0.0)
            kick = mass * rate * slip
            for x in range(reach):
                hi, lo = split2(kick * weights[x])
                pieces[v * reach + x] = hi
                pieces[(3 + v) * reach + x] = lo
        stripf = strip.astype(f32)
        for s in range(SOURCES):
            mask = short_rows(stripf[s : s + 1, :]) == strip_number
            for pair in range(3 * reach):
                both = [
                    jnp.broadcast_to(pieces[2 * pair + i, s : s + 1, :], (strips, capacity))
                    for i in range(2)
                ]
                leads[h][pair * 16 : (pair + 1) * 16, spans(s)] = jnp.where(
                    mask, jnp.concatenate(both, axis=0).astype(bf16), zero
                )

    def gather_up(h, keep):
        product = lax.dot_general(leads[h][...], onehots[h][...], NT, preferred_element_type=f32)
        product = product[:half] + product[half:]
        if keep is not None:
            product = jnp.where(keep, product, 0.0)
        total[...] = total[...] + product

    found = look_up(0)
    gather_up(1, step > 0)
    relax(0, *found)
    found = look_up(1)
    gather_up(0, None)
    relax(1, *found)

    @pl.when(step == pl.num_programs(0) - 1)
    def _():
        gather_up(1, None)

        def added(v, x):
            at = (v * reach + x) * strips
            return jnp.concatenate(
                [total[at : at + strips, h * LANES : (h + 1) * LANES] for h in range(2)], axis=0
            )

        for v in range(3):
            to_left_ref[4 + v] = added(v, 0)
            to_right_ref[4 + v] = added(v, width_x + 1)
            for x in range(width_x):
                raw_ref[v, x] = gas_ref[1 + v, x] + added(v, x + 1)
        to_other_ref[2 * width_x] = added(2, 0)
        to_other_ref[2 * width_x + 1] = added(2, width_x + 1)
        for x in range(width_x):
            pressure = sound_ref[x] * gas_ref[0, x]
            to_other_ref[x] = raw_ref[2, x]
            to_other_ref[width_x + x] = pressure
            if x < 2:
                to_left_ref[x] = pressure
                to_left_ref[2 + x] = raw_ref[0, x]
            if x >= width_x - 2:
                to_right_ref[x - width_x + 2] = pressure
                to_right_ref[x - width_x + 4] = raw_ref[0, x]


def deposit(arrived, gas, sound, count, capacity):
    pitch = arrived.shape[0] // count
    width_x, width_y, width_z = gas.shape[1:]
    reach = width_x + 2
    deposit_rows = 3 * reach * 8
    plane = (width_y, width_z)
    shapes = [(3, width_x) + plane, (7,) + plane, (7,) + plane, (2 * width_x + 2,) + plane]

    def whole(shape):
        return pl.BlockSpec(shape, lambda i: (0,) * len(shape))

    onehot = pltpu.VMEM((COLUMNS, SOURCES * capacity), jnp.bfloat16)
    lead = pltpu.VMEM((2 * deposit_rows, SOURCES * capacity), jnp.bfloat16)
    return pl.pallas_call(
        deposit_kernel,
        grid=(count // (2 * SOURCES),),
        in_specs=[
            pl.BlockSpec((2 * SOURCES * pitch, LANES), lambda i: (i, 0)),
            whole(gas.shape),
            whole(sound.shape),
        ],
        out_specs=[pl.BlockSpec((3, 2 * SOURCES, capacity), lambda i: (0, i, 0))]
        + [whole(shape) for shape in shapes],
        out_shape=[
            jax.ShapeDtypeStruct(shape, jnp.float32) for shape in [(3, count, capacity)] + shapes
        ],
        scratch_shapes=[
            pltpu.VMEM((6 * width_x * 8, COLUMNS), jnp.bfloat16),
            pltpu.VMEM((deposit_rows, COLUMNS), jnp.float32),
            onehot, onehot, lead, lead,
            pltpu.VMEM((3, SOURCES, capacity), jnp.float32),
            pltpu.VMEM((6 * reach, SOURCES, capacity), jnp.float32),
        ],
        compiler_params=pltpu.CompilerParams(vmem_limit_bytes=VMEM_BYTES),
        name="deposit",
    )(arrived, gas, sound)


def step_kernel(
    slab_ref, gas_ref, sound_ref, raw_ref, mine_left_ref, mine_right_ref,
    left_ref, right_ref, other_ref, next_ref,
):
    width_x, width_y, width_z = sound_ref.shape
    slab = slab_ref[0, 0]
    first_slab = slab == 0
    lane = lax.broadcasted_iota(jnp.int32, (width_y, width_z), 1)

    def along_y(f, shift):
        return pltpu.roll(f, (-shift) % width_y, 0)

    def along_z(f, other, shift):
        turned = pltpu.roll(f, (-shift) % width_z, 1)
        beyond = pltpu.roll(other, (-shift) % width_z, 1)
        if shift > 0:
            inside = lane < width_z - shift
            reached = first_slab
        else:
            inside = lane >= -shift
            reached = jnp.logical_not(first_slab)
        return jnp.where(inside, turned, jnp.where(reached, beyond, 0.0))

    def fourth(shifted):
        return (8.0 * (shifted(1) - shifted(-1)) - (shifted(2) - shifted(-2))) / 12.0

    def momentum(k, x):
        value = raw_ref[k, x]
        if x == 0:
            value = value + left_ref[4 + k]
        if x == width_x - 1:
            value = value + right_ref[4 + k]
        return value

    planes = [[momentum(k, x) for x in range(width_x)] for k in range(3)]
    first = {x: planes[0][x] for x in range(width_x)}
    first[-2] = left_ref[2]
    first[-1] = left_ref[3] + mine_left_ref[4]
    first[width_x] = right_ref[2] + mine_right_ref[4]
    first[width_x + 1] = right_ref[3]
    pressure = {x: sound_ref[x] * gas_ref[0, x] for x in range(width_x)}
    pressure[-2] = left_ref[0]
    pressure[-1] = left_ref[1]
    pressure[width_x] = right_ref[0]
    pressure[width_x + 1] = right_ref[1]
    for x in range(width_x):
        other = other_ref[x]
        if x == 0:
            other = other + left_ref[7]
        if x == width_x - 1:
            other = other + right_ref[7]
        other_p = other_ref[width_x + x]
        p = pressure[x]
        next_ref[0, x] = gas_ref[0, x] - courant * (
            fourth(lambda s: first[x + s])
            + fourth(lambda s: along_y(planes[1][x], s))
            + fourth(lambda s: along_z(planes[2][x], other, s))
        )
        next_ref[1, x] = planes[0][x] - courant * fourth(lambda s: pressure[x + s])
        next_ref[2, x] = planes[1][x] - courant * fourth(lambda s: along_y(p, s))
        next_ref[3, x] = planes[2][x] - courant * fourth(lambda s: along_z(p, other_p, s))


def gas_step(slab, gas, *rest):
    whole = pl.BlockSpec(memory_space=pltpu.VMEM)
    return pl.pallas_call(
        step_kernel,
        in_specs=[pl.BlockSpec(memory_space=pltpu.SMEM)] + [whole] * (1 + len(rest)),
        out_specs=whole,
        out_shape=jax.ShapeDtypeStruct(gas.shape, jnp.float32),
        compiler_params=pltpu.CompilerParams(vmem_limit_bytes=VMEM_BYTES),
        name="gas_step",
    )(slab, gas, *rest)


def per_device(
    gas_state, sound_speed, velocity, drag_rate, parcel_mass, cell_offset, target_owner,
    target_cell, live_counts,
):
    tiles = lax.axis_size("tile")
    slabs = lax.axis_size("slab")
    owner_count = tiles * slabs
    slot_count = target_cell.shape[-1]
    capacity = 3 * slot_count // (2 * owner_count)
    rows = slot_count // LANES
    width_x = gas_state.shape[1]
    to_right = [(t, (t + 1) % tiles) for t in range(tiles)]
    to_left = [(t, (t - 1) % tiles) for t in range(tiles)]
    swap = [(s, slabs - 1 - s) for s in range(slabs)]

    outbox = dispatch(
        live_counts,
        velocity.reshape(3, rows, LANES),
        drag_rate.reshape(rows, LANES),
        parcel_mass.reshape(rows, LANES),
        cell_offset.reshape(rows, LANES),
        target_owner.reshape(rows, LANES),
        target_cell.reshape(rows, LANES),
        owner_count,
        capacity,
    )
    arrived = lax.all_to_all(
        outbox.reshape(owner_count, 1, FIELDS * capacity), ("tile", "slab"),
        split_axis=0, concat_axis=0, tiled=True,
    ).reshape(outbox.shape)
    moved, raw, mine_right, mine_left, mine = deposit(
        arrived, gas_state, sound_speed, owner_count, capacity
    )
    other = lax.ppermute(mine, "slab", swap)
    left = lax.ppermute(
        jnp.concatenate([mine_right, other[2 * width_x + 1 :]]), "tile", to_right
    )
    right = lax.ppermute(
        jnp.concatenate([mine_left, other[2 * width_x : 2 * width_x + 1]]), "tile", to_left
    )
    slab = lax.axis_index("slab").astype(jnp.int32).reshape(1, 1)
    gas_next = gas_step(
        slab, gas_state, sound_speed, raw, mine_left, mine_right,
        left, right, other,
    )
    return gas_next, moved.reshape(3, 1, 1, owner_count, capacity)


def solution(mesh):
    return jax.shard_map(
        per_device,
        mesh=mesh,
        in_specs=(
            P(None, "tile", None, "slab"),
            P("tile", None, "slab"),
            P(None, "tile", "slab", None),
            P("tile", "slab", None),
            P("tile", "slab", None),
            P("tile", "slab", None),
            P("tile", "slab", None, None),
            P("tile", "slab", None),
            P("tile", "slab"),
        ),
        out_specs=(P(None, "tile", None, "slab"), P(None, "tile", "slab", None, None)),
        check_vma=False,
    )
```

```python
import jax
import jax.numpy as jnp
from jax import lax
from jax.experimental import pallas as pl
from jax.experimental.pallas import tpu as pltpu
from jax.sharding import PartitionSpec as P

courant = 0.4
LANES = 128
COLUMNS = 256
RES = 64
CHUNKS = 4
ROWS = 16
BLOCKS = 4
SOURCES = 8
FIELDS = 7
VMEM_BYTES = 40 * 1024 * 1024
NT = (((1,), (1,)), ((), ()))
NN = (((1,), (0,)), ((), ()))


def split2(x):
    hi = x.astype(jnp.bfloat16).astype(jnp.float32)
    return hi, x - hi


def dispatch_kernel(
    live_ref, vel_ref, rate_ref, mass_ref, off_ref, owner_ref, cell_ref, out_ref,
    acc, values, base, combined,
):
    owner_count = base.shape[0]
    windows = acc.shape[1]
    groups = acc.shape[2]
    pitch = out_ref.shape[0] // owner_count
    chunk = ROWS * LANES
    width = FIELDS * groups
    step = pl.program_id(0)
    f32, bf16 = jnp.float32, jnp.bfloat16

    @pl.when(step == 0)
    def _():
        acc[...] = jnp.zeros_like(acc)
        base[...] = jnp.zeros_like(base)

    def short_iota(rows):
        return lax.broadcasted_iota(jnp.int32, (rows, COLUMNS), 0).astype(f32).astype(bf16)

    def pair(x, t):
        return jnp.concatenate([x[2 * t : 2 * t + 1, :], x[2 * t + 1 : 2 * t + 2, :]], axis=1)

    def short_rows(row):
        return jnp.broadcast_to(row, (16, COLUMNS)).astype(bf16)

    one = jnp.ones((16, COLUMNS), bf16)
    zero = jnp.zeros((16, COLUMNS), bf16)

    def spread(row, rows):
        same = short_rows(row)
        numbers = short_iota(rows)
        return jnp.concatenate(
            [
                jnp.where(same == numbers[b * 16 : (b + 1) * 16], one, zero)
                for b in range(rows // 16)
            ],
            axis=0,
        )

    def multiply(group, picked, buffer):
        product = None
        numbers = short_iota(groups)
        for t in range(ROWS // 2):
            onehot = spread(pair(picked, t), COLUMNS)
            same = short_rows(pair(group, t))
            masks = [same == numbers[b * 16 : (b + 1) * 16] for b in range(groups // 16)]
            blocks = []
            for v in range(2 * FIELDS):
                value = short_rows(pair(values[buffer, v], t))
                for mask in masks:
                    blocks.append(jnp.where(mask, value, zero))
            part = lax.dot_general(
                jnp.concatenate(blocks, axis=0), onehot, NT, preferred_element_type=f32
            )
            product = part if product is None else product + part
        return product

    def add_product(product, start, number):
        product = product[:width] + product[width:]
        starts = start.astype(jnp.int32)
        lane = lax.broadcasted_iota(jnp.int32, (groups, LANES), 1)
        for k in range(COLUMNS // LANES):
            cols = slice(k * LANES, (k + 1) * LANES)
            even = starts[2 * k * groups : (2 * k + 1) * groups]
            odd = starts[(2 * k + 1) * groups : (2 * k + 2) * groups]
            first = jnp.where(lane < RES, even, odd) + number * RES
            window = (first + (((lane & (RES - 1)) - first) & (RES - 1))) >> 6
            for w in range(windows):
                here = window == w
                for v in range(FIELDS):
                    acc[v, w, :, cols] += jnp.where(
                        here, product[v * groups : (v + 1) * groups, cols], 0.0
                    )

    before = lax.broadcasted_iota(jnp.int32, (COLUMNS, COLUMNS + LANES), 0)
    after = lax.broadcasted_iota(jnp.int32, (COLUMNS, COLUMNS + LANES), 1)
    upper = jnp.where(before < after, 1.0, 0.0).astype(bf16)
    owner_row = lax.broadcasted_iota(jnp.int32, (owner_count, LANES), 0)

    def rank_slots(h):
        part = slice(h * ROWS, (h + 1) * ROWS)
        slot = (
            (CHUNKS * step + h) * chunk
            + lax.broadcasted_iota(jnp.int32, (ROWS, LANES), 0) * LANES
            + lax.broadcasted_iota(jnp.int32, (ROWS, LANES), 1)
        )
        alive = slot < live_ref[0, 0]
        dest = jnp.where(alive, owner_ref[part], owner_count)
        destf = dest.astype(f32)
        start = base[...]
        running = start * float(chunk)
        owners = jnp.concatenate(
            [spread(pair(destf, t), owner_count) for t in range(ROWS // 2)], axis=0
        )
        priors = lax.dot_general(owners, upper, NN, preferred_element_type=f32)
        for t in range(ROWS // 2):
            prior = priors[t * owner_count : (t + 1) * owner_count]
            for half in range(2):
                j = 2 * t + half
                total = prior[:, half * LANES : (half + 1) * LANES] + running
                combined[j : j + 1, :] = jnp.sum(
                    jnp.where(dest[j : j + 1, :] == owner_row, total, 0.0), axis=0, keepdims=True
                )
            running = running + prior[:, COLUMNS:]
        tally = running - start * float(chunk)
        base[...] = start + tally
        both = combined[...].astype(jnp.int32)
        local_rank = both & (chunk - 1)
        rank = local_rank + (both >> 11)
        column = (dest // groups) * RES + (rank & (RES - 1))
        turn = jnp.where(alive, local_rank >> 6, -1)
        fields = [
            vel_ref[0, part], vel_ref[1, part], vel_ref[2, part], rate_ref[part], mass_ref[part],
            off_ref[part], cell_ref[part].astype(f32),
        ]
        for v, field in enumerate(fields):
            hi, lo = split2(field)
            values[h, v] = hi
            values[h, v + FIELDS] = lo
        group = (dest & (groups - 1)).astype(f32)
        passes = (jnp.max(tally).astype(jnp.int32) + RES - 1) >> 6
        return passes, turn, column, group, start

    def one_pass(h, state, number):
        _, turn, column, group, start = state
        picked = jnp.where(turn == number, column, -1).astype(f32)
        add_product(multiply(group, picked, h), start, number)

    states = [rank_slots(h) for h in range(CHUNKS)]
    for h in range(CHUNKS):
        one_pass(h, states[h], 0)
    for h in range(CHUNKS):
        @pl.when(states[h][0] > 1)
        def _():
            def body(number, carry):
                one_pass(h, states[h], number)
                return carry

            lax.fori_loop(1, states[h][0], body, 0)

    @pl.when(step == pl.num_programs(0) - 1)
    def _():
        low = lax.broadcasted_iota(jnp.int32, (8, LANES), 1) < RES
        for v in range(FIELDS):
            for k in range(COLUMNS // LANES):
                cols = slice(k * LANES, (k + 1) * LANES)
                for m in range(windows // 2):
                    for part in range(groups // 8):
                        rows = slice(part * 8, (part + 1) * 8)
                        near = acc[v, 2 * m, rows, cols]
                        far = acc[v, 2 * m + 1, rows, cols]
                        place = v * (windows // 2) + m
                        even = (2 * k * groups + part * 8) * pitch + place
                        odd = ((2 * k + 1) * groups + part * 8) * pitch + place
                        out_ref[pl.ds(even, 8, stride=pitch), :] = jnp.where(
                            low, near, pltpu.roll(far, RES, 1)
                        )
                        out_ref[pl.ds(odd, 8, stride=pitch), :] = jnp.where(
                            low, pltpu.roll(near, RES, 1), far
                        )


def dispatch(live, vel, rate, mass, off, owner, cell, owner_count, capacity):
    rows = rate.shape[0]
    groups = owner_count * RES // COLUMNS
    pitch = FIELDS * capacity // LANES
    plain = pl.BlockSpec((CHUNKS * ROWS, LANES), lambda i: (i, 0))
    return pl.pallas_call(
        dispatch_kernel,
        grid=(rows // (CHUNKS * ROWS),),
        in_specs=[
            pl.BlockSpec(memory_space=pltpu.SMEM),
            pl.BlockSpec((3, CHUNKS * ROWS, LANES), lambda i: (0, i, 0)),
            plain, plain, plain, plain, plain,
        ],
        out_specs=pl.BlockSpec((owner_count * pitch, LANES), lambda i: (0, 0)),
        out_shape=jax.ShapeDtypeStruct((owner_count * pitch, LANES), jnp.float32),
        scratch_shapes=[
            pltpu.VMEM((FIELDS, capacity // RES, groups, COLUMNS), jnp.float32),
            pltpu.VMEM((CHUNKS, 2 * FIELDS, ROWS, LANES), jnp.float32),
            pltpu.VMEM((owner_count, LANES), jnp.float32),
            pltpu.VMEM((ROWS, LANES), jnp.float32),
        ],
        compiler_params=pltpu.CompilerParams(vmem_limit_bytes=60 * 1024 * 1024),
        name="dispatch",
    )(live, vel, rate, mass, off, owner, cell)


def deposit_kernel(
    arrived_ref, gas_ref, sound_ref,
    moved_ref, raw_ref, to_right_ref, to_left_ref, to_other_ref,
    table, total, speeds, pieces,
):
    capacity = moved_ref.shape[2]
    width_x = gas_ref.shape[1]
    reach = width_x + 2
    strips = 8
    rows = width_x * strips
    half = 3 * reach * strips
    pitch = arrived_ref.shape[0] // (BLOCKS * SOURCES)
    parts = capacity // LANES
    units = [(s, m) for m in range(parts) for s in range(SOURCES)]
    f32, bf16 = jnp.float32, jnp.bfloat16
    step = pl.program_id(0)

    @pl.when(step == 0)
    def _():
        total[...] = jnp.zeros_like(total)
        for v in range(3):
            for x in range(0, width_x, 2):
                for h in range(2):
                    two = [gas_ref[1 + v, x + i, h * 8 : (h + 1) * 8, :] for i in range(2)]
                    hi, lo = split2(jnp.concatenate(two, axis=0))
                    at = v * rows + x * strips
                    cols = slice(h * LANES, (h + 1) * LANES)
                    table[at : at + 16, cols] = hi.astype(bf16)
                    table[3 * rows + at : 3 * rows + at + 16, cols] = lo.astype(bf16)

    one = jnp.ones((16, COLUMNS), bf16)
    zero = jnp.zeros((16, COLUMNS), bf16)
    number = lax.broadcasted_iota(jnp.int32, (16, COLUMNS), 0)
    numbers = [(number + 16 * b).astype(f32).astype(bf16) for b in range(COLUMNS // 16)]
    strip_number = (number & (strips - 1)).astype(f32).astype(bf16)
    row_row = lax.broadcasted_iota(jnp.int32, (rows, LANES), 0)

    def cut(x, unit):
        s, m = unit
        return x[s : s + 1, m * LANES : (m + 1) * LANES]

    def pair(x, u):
        return jnp.concatenate([cut(x, units[u]), cut(x, units[u + 1])], axis=1)

    def short_rows(row):
        return jnp.broadcast_to(row, (16, COLUMNS)).astype(bf16)

    def spread(column, u):
        same = short_rows(pair(column, u))
        return jnp.concatenate([jnp.where(same == n, one, zero) for n in numbers], axis=0)

    def field(h, v):
        first = h * SOURCES * pitch + v * parts
        return jnp.concatenate(
            [arrived_ref[pl.ds(first + m, SOURCES, stride=pitch), :] for m in range(parts)], axis=1
        )

    def look_up(h):
        cell = field(h, 6).astype(jnp.int32)
        column = ((cell & (LANES - 1)) + ((cell >> 10) & 1) * LANES).astype(f32)
        strip = (cell >> 7) & (strips - 1)
        row = (cell >> 11) * strips + strip
        for u in range(0, len(units), 2):
            found = lax.dot_general(
                table[...], spread(column, u), NN, preferred_element_type=f32
            )
            found = found[: 3 * rows] + found[3 * rows :]
            for i in range(2):
                s, m = units[u + i]
                mask = cut(row, units[u + i]) == row_row
                for v in range(3):
                    mine = found[v * rows : (v + 1) * rows, i * LANES : (i + 1) * LANES]
                    speeds[h, v, s : s + 1, m * LANES : (m + 1) * LANES] = jnp.sum(
                        jnp.where(mask, mine, 0.0), axis=0, keepdims=True
                    )
        return cell, column, strip.astype(f32)

    def relax(h, cell):
        part = slice(h * SOURCES, (h + 1) * SOURCES)
        plane = cell >> 11
        rate = field(h, 3)
        mass = field(h, 4)
        shift = field(h, 5)
        occupied = mass > 0.0
        low_weight = 0.5 * (0.5 - shift) ** 2
        mid_weight = 0.75 - shift**2
        high_weight = 0.5 * (0.5 + shift) ** 2
        weights = []
        for x in range(reach):
            rest = jnp.where(plane == x - 2, high_weight, 0.0)
            rest = jnp.where(plane == x - 1, mid_weight, rest)
            weights.append(jnp.where(plane == x, low_weight, rest))
        for v in range(3):
            speed = field(h, v)
            slip = speed - speeds[h, v]
            moved_ref[v, part] = jnp.where(occupied, speed - rate * slip, 0.0)
            kick = mass * rate * slip
            for x in range(reach):
                hi, lo = split2(kick * weights[x])
                pieces[h, v * reach + x] = hi
                pieces[h, (3 + v) * reach + x] = lo

    def gather_up(h, column, strip):
        product = None
        for u in range(0, len(units), 2):
            mask = short_rows(pair(strip, u)) == strip_number
            blocks = []
            for p in range(3 * reach):
                both = [
                    jnp.broadcast_to(pair(pieces[h, 2 * p + i], u), (strips, COLUMNS))
                    for i in range(2)
                ]
                blocks.append(jnp.where(mask, jnp.concatenate(both, axis=0).astype(bf16), zero))
            part = lax.dot_general(
                jnp.concatenate(blocks, axis=0), spread(column, u), NT, preferred_element_type=f32
            )
            product = part if product is None else product + part
        total[...] = total[...] + (product[:half] + product[half:])

    found = [look_up(h) for h in range(BLOCKS)]
    for h in range(BLOCKS):
        relax(h, found[h][0])
    for h in range(BLOCKS):
        gather_up(h, *found[h][1:])

    @pl.when(step == pl.num_programs(0) - 1)
    def _():
        def added(v, x):
            at = (v * reach + x) * strips
            return jnp.concatenate(
                [total[at : at + strips, h * LANES : (h + 1) * LANES] for h in range(2)], axis=0
            )

        for v in range(3):
            to_left_ref[4 + v] = added(v, 0)
            to_right_ref[4 + v] = added(v, width_x + 1)
            for x in range(width_x):
                raw_ref[v, x] = gas_ref[1 + v, x] + added(v, x + 1)
        to_other_ref[2 * width_x] = added(2, 0)
        to_other_ref[2 * width_x + 1] = added(2, width_x + 1)
        for x in range(width_x):
            pressure = sound_ref[x] * gas_ref[0, x]
            to_other_ref[x] = raw_ref[2, x]
            to_other_ref[width_x + x] = pressure
            if x < 2:
                to_left_ref[x] = pressure
                to_left_ref[2 + x] = raw_ref[0, x]
            if x >= width_x - 2:
                to_right_ref[x - width_x + 2] = pressure
                to_right_ref[x - width_x + 4] = raw_ref[0, x]


def deposit(arrived, gas, sound, count, capacity):
    pitch = arrived.shape[0] // count
    width_x, width_y, width_z = gas.shape[1:]
    reach = width_x + 2
    deposit_rows = 3 * reach * 8
    plane = (width_y, width_z)
    shapes = [(3, width_x) + plane, (7,) + plane, (7,) + plane, (2 * width_x + 2,) + plane]

    def whole(shape):
        return pl.BlockSpec(shape, lambda i: (0,) * len(shape))

    return pl.pallas_call(
        deposit_kernel,
        grid=(count // (BLOCKS * SOURCES),),
        in_specs=[
            pl.BlockSpec((BLOCKS * SOURCES * pitch, LANES), lambda i: (i, 0)),
            whole(gas.shape),
            whole(sound.shape),
        ],
        out_specs=[pl.BlockSpec((3, BLOCKS * SOURCES, capacity), lambda i: (0, i, 0))]
        + [whole(shape) for shape in shapes],
        out_shape=[
            jax.ShapeDtypeStruct(shape, jnp.float32) for shape in [(3, count, capacity)] + shapes
        ],
        scratch_shapes=[
            pltpu.VMEM((6 * width_x * 8, COLUMNS), jnp.bfloat16),
            pltpu.VMEM((deposit_rows, COLUMNS), jnp.float32),
            pltpu.VMEM((BLOCKS, 3, SOURCES, capacity), jnp.float32),
            pltpu.VMEM((BLOCKS, 6 * reach, SOURCES, capacity), jnp.float32),
        ],
        compiler_params=pltpu.CompilerParams(vmem_limit_bytes=VMEM_BYTES),
        name="deposit",
    )(arrived, gas, sound)


def step_kernel(
    slab_ref, gas_ref, sound_ref, raw_ref, mine_left_ref, mine_right_ref,
    left_ref, right_ref, other_ref, next_ref,
):
    width_x, width_y, width_z = sound_ref.shape
    slab = slab_ref[0, 0]
    first_slab = slab == 0
    lane = lax.broadcasted_iota(jnp.int32, (width_y, width_z), 1)

    def along_y(f, shift):
        return pltpu.roll(f, (-shift) % width_y, 0)

    def along_z(f, other, shift):
        turned = pltpu.roll(f, (-shift) % width_z, 1)
        beyond = pltpu.roll(other, (-shift) % width_z, 1)
        if shift > 0:
            inside = lane < width_z - shift
            reached = first_slab
        else:
            inside = lane >= -shift
            reached = jnp.logical_not(first_slab)
        return jnp.where(inside, turned, jnp.where(reached, beyond, 0.0))

    def fourth(shifted):
        return (8.0 * (shifted(1) - shifted(-1)) - (shifted(2) - shifted(-2))) / 12.0

    def momentum(k, x):
        value = raw_ref[k, x]
        if x == 0:
            value = value + left_ref[4 + k]
        if x == width_x - 1:
            value = value + right_ref[4 + k]
        return value

    planes = [[momentum(k, x) for x in range(width_x)] for k in range(3)]
    first = {x: planes[0][x] for x in range(width_x)}
    first[-2] = left_ref[2]
    first[-1] = left_ref[3] + mine_left_ref[4]
    first[width_x] = right_ref[2] + mine_right_ref[4]
    first[width_x + 1] = right_ref[3]
    pressure = {x: sound_ref[x] * gas_ref[0, x] for x in range(width_x)}
    pressure[-2] = left_ref[0]
    pressure[-1] = left_ref[1]
    pressure[width_x] = right_ref[0]
    pressure[width_x + 1] = right_ref[1]
    for x in range(width_x):
        other = other_ref[x]
        if x == 0:
            other = other + left_ref[7]
        if x == width_x - 1:
            other = other + right_ref[7]
        other_p = other_ref[width_x + x]
        p = pressure[x]
        next_ref[0, x] = gas_ref[0, x] - courant * (
            fourth(lambda s: first[x + s])
            + fourth(lambda s: along_y(planes[1][x], s))
            + fourth(lambda s: along_z(planes[2][x], other, s))
        )
        next_ref[1, x] = planes[0][x] - courant * fourth(lambda s: pressure[x + s])
        next_ref[2, x] = planes[1][x] - courant * fourth(lambda s: along_y(p, s))
        next_ref[3, x] = planes[2][x] - courant * fourth(lambda s: along_z(p, other_p, s))


def gas_step(slab, gas, *rest):
    whole = pl.BlockSpec(memory_space=pltpu.VMEM)
    return pl.pallas_call(
        step_kernel,
        in_specs=[pl.BlockSpec(memory_space=pltpu.SMEM)] + [whole] * (1 + len(rest)),
        out_specs=whole,
        out_shape=jax.ShapeDtypeStruct(gas.shape, jnp.float32),
        compiler_params=pltpu.CompilerParams(vmem_limit_bytes=VMEM_BYTES),
        name="gas_step",
    )(slab, gas, *rest)


def per_device(
    gas_state, sound_speed, velocity, drag_rate, parcel_mass, cell_offset, target_owner,
    target_cell, live_counts,
):
    tiles = lax.axis_size("tile")
    slabs = lax.axis_size("slab")
    owner_count = tiles * slabs
    slot_count = target_cell.shape[-1]
    capacity = 3 * slot_count // (2 * owner_count)
    rows = slot_count // LANES
    width_x = gas_state.shape[1]
    to_right = [(t, (t + 1) % tiles) for t in range(tiles)]
    to_left = [(t, (t - 1) % tiles) for t in range(tiles)]
    swap = [(s, slabs - 1 - s) for s in range(slabs)]

    outbox = dispatch(
        live_counts,
        velocity.reshape(3, rows, LANES),
        drag_rate.reshape(rows, LANES),
        parcel_mass.reshape(rows, LANES),
        cell_offset.reshape(rows, LANES),
        target_owner.reshape(rows, LANES),
        target_cell.reshape(rows, LANES),
        owner_count,
        capacity,
    )
    arrived = lax.all_to_all(
        outbox.reshape(owner_count, 1, FIELDS * capacity), ("tile", "slab"),
        split_axis=0, concat_axis=0, tiled=True,
    ).reshape(outbox.shape)
    moved, raw, mine_right, mine_left, mine = deposit(
        arrived, gas_state, sound_speed, owner_count, capacity
    )
    other = lax.ppermute(mine, "slab", swap)
    left = lax.ppermute(
        jnp.concatenate([mine_right, other[2 * width_x + 1 :]]), "tile", to_right
    )
    right = lax.ppermute(
        jnp.concatenate([mine_left, other[2 * width_x : 2 * width_x + 1]]), "tile", to_left
    )
    slab = lax.axis_index("slab").astype(jnp.int32).reshape(1, 1)
    gas_next = gas_step(
        slab, gas_state, sound_speed, raw, mine_left, mine_right,
        left, right, other,
    )
    return gas_next, moved.reshape(3, 1, 1, owner_count, capacity)


def solution(mesh):
    return jax.shard_map(
        per_device,
        mesh=mesh,
        in_specs=(
            P(None, "tile", None, "slab"),
            P("tile", None, "slab"),
            P(None, "tile", "slab", None),
            P("tile", "slab", None),
            P("tile", "slab", None),
            P("tile", "slab", None),
            P("tile", "slab", None, None),
            P("tile", "slab", None),
            P("tile", "slab"),
        ),
        out_specs=(P(None, "tile", None, "slab"), P(None, "tile", "slab", None, None)),
        check_vma=False,
    )
```

```python
import jax
import jax.numpy as jnp
from jax import lax
from jax.experimental import pallas as pl
from jax.experimental.pallas import tpu as pltpu
from jax.sharding import PartitionSpec as P

courant = 0.4
LANES = 128
COLUMNS = 256
RES = 64
CHUNKS = 4
ROWS = 16
BLOCKS = 8
SOURCES = 8
FIELDS = 7
VMEM_BYTES = 40 * 1024 * 1024
COUNTED = jnp.float8_e4m3fn
NT = (((1,), (1,)), ((), ()))
NN = (((1,), (0,)), ((), ()))


def split2(x):
    hi = x.astype(jnp.bfloat16).astype(jnp.float32)
    return hi, x - hi


def dispatch_kernel(
    live_ref, vel_ref, rate_ref, mass_ref, off_ref, owner_ref, cell_ref, out_ref,
    acc, values, base, combined,
):
    owner_count = base.shape[0]
    windows = acc.shape[1]
    groups = acc.shape[2]
    pitch = out_ref.shape[0] // owner_count
    chunk = ROWS * LANES
    width = FIELDS * groups
    step = pl.program_id(0)
    f32, bf16 = jnp.float32, jnp.bfloat16

    @pl.when(step == 0)
    def _():
        acc[...] = jnp.zeros_like(acc)
        base[...] = jnp.zeros_like(base)

    def short_iota(rows):
        return lax.broadcasted_iota(jnp.int32, (rows, COLUMNS), 0).astype(f32).astype(bf16)

    def pair(x, t):
        return jnp.concatenate([x[2 * t : 2 * t + 1, :], x[2 * t + 1 : 2 * t + 2, :]], axis=1)

    def short_rows(row):
        return jnp.broadcast_to(row, (16, COLUMNS)).astype(bf16)

    one = jnp.ones((16, COLUMNS), bf16)
    zero = jnp.zeros((16, COLUMNS), bf16)

    def spread(row, rows):
        same = short_rows(row)
        numbers = short_iota(rows)
        return jnp.concatenate(
            [
                jnp.where(same == numbers[b * 16 : (b + 1) * 16], one, zero)
                for b in range(rows // 16)
            ],
            axis=0,
        )

    def multiply(group, picked, buffer):
        product = None
        numbers = short_iota(groups)
        for t in range(ROWS // 2):
            onehot = spread(pair(picked, t), COLUMNS)
            same = short_rows(pair(group, t))
            masks = [same == numbers[b * 16 : (b + 1) * 16] for b in range(groups // 16)]
            blocks = []
            for v in range(2 * FIELDS):
                value = short_rows(pair(values[buffer, v], t))
                for mask in masks:
                    blocks.append(jnp.where(mask, value, zero))
            part = lax.dot_general(
                jnp.concatenate(blocks, axis=0), onehot, NT, preferred_element_type=f32
            )
            product = part if product is None else product + part
        return product

    def add_product(product, start, number):
        product = product[:width] + product[width:]
        starts = start.astype(jnp.int32)
        lane = lax.broadcasted_iota(jnp.int32, (groups, LANES), 1)
        for k in range(COLUMNS // LANES):
            cols = slice(k * LANES, (k + 1) * LANES)
            even = starts[2 * k * groups : (2 * k + 1) * groups]
            odd = starts[(2 * k + 1) * groups : (2 * k + 2) * groups]
            first = jnp.where(lane < RES, even, odd) + number * RES
            window = (first + (((lane & (RES - 1)) - first) & (RES - 1))) >> 6
            for w in range(windows):
                here = window == w
                for v in range(FIELDS):
                    acc[v, w, :, cols] += jnp.where(
                        here, product[v * groups : (v + 1) * groups, cols], 0.0
                    )

    before = lax.broadcasted_iota(jnp.int32, (COLUMNS, COLUMNS), 0)
    after = lax.broadcasted_iota(jnp.int32, (COLUMNS, COLUMNS), 1)
    upper = jnp.where(before <= after, 1.0, 0.0).astype(COUNTED)
    owner_row = lax.broadcasted_iota(jnp.int32, (owner_count, LANES), 0)

    def rank_slots(h):
        part = slice(h * ROWS, (h + 1) * ROWS)
        slot = (
            (CHUNKS * step + h) * chunk
            + lax.broadcasted_iota(jnp.int32, (ROWS, LANES), 0) * LANES
            + lax.broadcasted_iota(jnp.int32, (ROWS, LANES), 1)
        )
        alive = slot < live_ref[0, 0]
        dest = jnp.where(alive, owner_ref[part], owner_count)
        destf = dest.astype(f32)
        start = base[...]
        running = start * float(chunk)
        owners = jnp.concatenate(
            [spread(pair(destf, t), owner_count) for t in range(ROWS // 2)], axis=0
        )
        priors = lax.dot_general(owners.astype(COUNTED), upper, NN, preferred_element_type=f32)
        for t in range(ROWS // 2):
            prior = priors[t * owner_count : (t + 1) * owner_count]
            for half in range(2):
                j = 2 * t + half
                total = prior[:, half * LANES : (half + 1) * LANES] + running
                combined[j : j + 1, :] = jnp.sum(
                    jnp.where(dest[j : j + 1, :] == owner_row, total, 0.0), axis=0, keepdims=True
                )
            running = running + jnp.broadcast_to(prior[:, COLUMNS - 1 :], (owner_count, LANES))
        tally = running - start * float(chunk)
        base[...] = start + tally
        both = combined[...].astype(jnp.int32) - 1
        local_rank = both & (chunk - 1)
        rank = local_rank + (both >> 11)
        column = (dest // groups) * RES + (rank & (RES - 1))
        turn = jnp.where(alive, local_rank >> 6, -1)
        fields = [
            vel_ref[0, part], vel_ref[1, part], vel_ref[2, part], rate_ref[part], mass_ref[part],
            off_ref[part], cell_ref[part].astype(f32),
        ]
        for v, field in enumerate(fields):
            hi, lo = split2(field)
            values[h, v] = hi
            values[h, v + FIELDS] = lo
        group = (dest & (groups - 1)).astype(f32)
        passes = (jnp.max(tally).astype(jnp.int32) + RES - 1) >> 6
        return passes, turn, column, group, start

    def one_pass(h, state, number):
        _, turn, column, group, start = state
        picked = jnp.where(turn == number, column, -1).astype(f32)
        add_product(multiply(group, picked, h), start, number)

    states = [rank_slots(h) for h in range(CHUNKS)]
    for h in range(CHUNKS):
        one_pass(h, states[h], 0)
    for h in range(CHUNKS):
        @pl.when(states[h][0] > 1)
        def _():
            def body(number, carry):
                one_pass(h, states[h], number)
                return carry

            lax.fori_loop(1, states[h][0], body, 0)

    @pl.when(step == pl.num_programs(0) - 1)
    def _():
        low = lax.broadcasted_iota(jnp.int32, (8, LANES), 1) < RES
        for v in range(FIELDS):
            for k in range(COLUMNS // LANES):
                cols = slice(k * LANES, (k + 1) * LANES)
                for m in range(windows // 2):
                    for part in range(groups // 8):
                        rows = slice(part * 8, (part + 1) * 8)
                        near = acc[v, 2 * m, rows, cols]
                        far = acc[v, 2 * m + 1, rows, cols]
                        place = v * (windows // 2) + m
                        even = (2 * k * groups + part * 8) * pitch + place
                        odd = ((2 * k + 1) * groups + part * 8) * pitch + place
                        out_ref[pl.ds(even, 8, stride=pitch), :] = jnp.where(
                            low, near, pltpu.roll(far, RES, 1)
                        )
                        out_ref[pl.ds(odd, 8, stride=pitch), :] = jnp.where(
                            low, pltpu.roll(near, RES, 1), far
                        )


def dispatch(live, vel, rate, mass, off, owner, cell, owner_count, capacity):
    rows = rate.shape[0]
    groups = owner_count * RES // COLUMNS
    pitch = FIELDS * capacity // LANES
    plain = pl.BlockSpec((CHUNKS * ROWS, LANES), lambda i: (i, 0))
    return pl.pallas_call(
        dispatch_kernel,
        grid=(rows // (CHUNKS * ROWS),),
        in_specs=[
            pl.BlockSpec(memory_space=pltpu.SMEM),
            pl.BlockSpec((3, CHUNKS * ROWS, LANES), lambda i: (0, i, 0)),
            plain, plain, plain, plain, plain,
        ],
        out_specs=pl.BlockSpec((owner_count * pitch, LANES), lambda i: (0, 0)),
        out_shape=jax.ShapeDtypeStruct((owner_count * pitch, LANES), jnp.float32),
        scratch_shapes=[
            pltpu.VMEM((FIELDS, capacity // RES, groups, COLUMNS), jnp.float32),
            pltpu.VMEM((CHUNKS, 2 * FIELDS, ROWS, LANES), jnp.float32),
            pltpu.VMEM((owner_count, LANES), jnp.float32),
            pltpu.VMEM((ROWS, LANES), jnp.float32),
        ],
        compiler_params=pltpu.CompilerParams(vmem_limit_bytes=60 * 1024 * 1024),
        name="dispatch",
    )(live, vel, rate, mass, off, owner, cell)


def deposit_kernel(
    arrived_ref, gas_ref, sound_ref,
    moved_ref, raw_ref, to_right_ref, to_left_ref, to_other_ref,
    table, total, speeds, pieces,
):
    capacity = moved_ref.shape[2]
    width_x = gas_ref.shape[1]
    reach = width_x + 2
    strips = 8
    rows = width_x * strips
    half = 3 * reach * strips
    pitch = arrived_ref.shape[0] // (BLOCKS * SOURCES)
    parts = capacity // LANES
    units = [(s, m) for m in range(parts) for s in range(SOURCES)]
    f32, bf16 = jnp.float32, jnp.bfloat16
    step = pl.program_id(0)

    @pl.when(step == 0)
    def _():
        total[...] = jnp.zeros_like(total)
        for v in range(3):
            for x in range(0, width_x, 2):
                for h in range(2):
                    two = [gas_ref[1 + v, x + i, h * 8 : (h + 1) * 8, :] for i in range(2)]
                    hi, lo = split2(jnp.concatenate(two, axis=0))
                    at = v * rows + x * strips
                    cols = slice(h * LANES, (h + 1) * LANES)
                    table[at : at + 16, cols] = hi.astype(bf16)
                    table[3 * rows + at : 3 * rows + at + 16, cols] = lo.astype(bf16)

    one = jnp.ones((16, COLUMNS), bf16)
    zero = jnp.zeros((16, COLUMNS), bf16)
    number = lax.broadcasted_iota(jnp.int32, (16, COLUMNS), 0)
    numbers = [(number + 16 * b).astype(f32).astype(bf16) for b in range(COLUMNS // 16)]
    strip_number = (number & (strips - 1)).astype(f32).astype(bf16)
    row_row = lax.broadcasted_iota(jnp.int32, (rows, LANES), 0)

    def cut(x, unit):
        s, m = unit
        return x[s : s + 1, m * LANES : (m + 1) * LANES]

    def pair(x, u):
        return jnp.concatenate([cut(x, units[u]), cut(x, units[u + 1])], axis=1)

    def short_rows(row):
        return jnp.broadcast_to(row, (16, COLUMNS)).astype(bf16)

    def spread(column, u):
        same = short_rows(pair(column, u))
        return jnp.concatenate([jnp.where(same == n, one, zero) for n in numbers], axis=0)

    def field(h, v):
        first = h * SOURCES * pitch + v * parts
        return jnp.concatenate(
            [arrived_ref[pl.ds(first + m, SOURCES, stride=pitch), :] for m in range(parts)], axis=1
        )

    def look_up(h):
        cell = field(h, 6).astype(jnp.int32)
        column = ((cell & (LANES - 1)) + ((cell >> 10) & 1) * LANES).astype(f32)
        strip = (cell >> 7) & (strips - 1)
        row = (cell >> 11) * strips + strip
        for u in range(0, len(units), 2):
            found = lax.dot_general(
                table[...], spread(column, u), NN, preferred_element_type=f32
            )
            found = found[: 3 * rows] + found[3 * rows :]
            for i in range(2):
                s, m = units[u + i]
                mask = cut(row, units[u + i]) == row_row
                for v in range(3):
                    mine = found[v * rows : (v + 1) * rows, i * LANES : (i + 1) * LANES]
                    speeds[h, v, s : s + 1, m * LANES : (m + 1) * LANES] = jnp.sum(
                        jnp.where(mask, mine, 0.0), axis=0, keepdims=True
                    )
        return cell, column, strip.astype(f32)

    def relax(h, cell):
        part = slice(h * SOURCES, (h + 1) * SOURCES)
        plane = cell >> 11
        rate = field(h, 3)
        mass = field(h, 4)
        shift = field(h, 5)
        occupied = mass > 0.0
        low_weight = 0.5 * (0.5 - shift) ** 2
        mid_weight = 0.75 - shift**2
        high_weight = 0.5 * (0.5 + shift) ** 2
        weights = []
        for x in range(reach):
            rest = jnp.where(plane == x - 2, high_weight, 0.0)
            rest = jnp.where(plane == x - 1, mid_weight, rest)
            weights.append(jnp.where(plane == x, low_weight, rest))
        for v in range(3):
            speed = field(h, v)
            slip = speed - speeds[h, v]
            moved_ref[v, part] = jnp.where(occupied, speed - rate * slip, 0.0)
            kick = mass * rate * slip
            for x in range(reach):
                hi, lo = split2(kick * weights[x])
                pieces[h, v * reach + x] = hi
                pieces[h, (3 + v) * reach + x] = lo

    def gather_up(h, column, strip):
        product = None
        for u in range(0, len(units), 2):
            mask = short_rows(pair(strip, u)) == strip_number
            blocks = []
            for p in range(3 * reach):
                both = [
                    jnp.broadcast_to(pair(pieces[h, 2 * p + i], u), (strips, COLUMNS))
                    for i in range(2)
                ]
                blocks.append(jnp.where(mask, jnp.concatenate(both, axis=0).astype(bf16), zero))
            part = lax.dot_general(
                jnp.concatenate(blocks, axis=0), spread(column, u), NT, preferred_element_type=f32
            )
            product = part if product is None else product + part
        total[...] = total[...] + (product[:half] + product[half:])

    found = [look_up(h) for h in range(BLOCKS)]
    for h in range(BLOCKS):
        relax(h, found[h][0])
    for h in range(BLOCKS):
        gather_up(h, *found[h][1:])

    @pl.when(step == pl.num_programs(0) - 1)
    def _():
        def added(v, x):
            at = (v * reach + x) * strips
            return jnp.concatenate(
                [total[at : at + strips, h * LANES : (h + 1) * LANES] for h in range(2)], axis=0
            )

        for v in range(3):
            to_left_ref[4 + v] = added(v, 0)
            to_right_ref[4 + v] = added(v, width_x + 1)
            for x in range(width_x):
                raw_ref[v, x] = gas_ref[1 + v, x] + added(v, x + 1)
        to_other_ref[2 * width_x] = added(2, 0)
        to_other_ref[2 * width_x + 1] = added(2, width_x + 1)
        for x in range(width_x):
            pressure = sound_ref[x] * gas_ref[0, x]
            to_other_ref[x] = raw_ref[2, x]
            to_other_ref[width_x + x] = pressure
            if x < 2:
                to_left_ref[x] = pressure
                to_left_ref[2 + x] = raw_ref[0, x]
            if x >= width_x - 2:
                to_right_ref[x - width_x + 2] = pressure
                to_right_ref[x - width_x + 4] = raw_ref[0, x]


def deposit(arrived, gas, sound, count, capacity):
    pitch = arrived.shape[0] // count
    width_x, width_y, width_z = gas.shape[1:]
    reach = width_x + 2
    deposit_rows = 3 * reach * 8
    plane = (width_y, width_z)
    shapes = [(3, width_x) + plane, (7,) + plane, (7,) + plane, (2 * width_x + 2,) + plane]

    def whole(shape):
        return pl.BlockSpec(shape, lambda i: (0,) * len(shape))

    return pl.pallas_call(
        deposit_kernel,
        grid=(count // (BLOCKS * SOURCES),),
        in_specs=[
            pl.BlockSpec((BLOCKS * SOURCES * pitch, LANES), lambda i: (i, 0)),
            whole(gas.shape),
            whole(sound.shape),
        ],
        out_specs=[pl.BlockSpec((3, BLOCKS * SOURCES, capacity), lambda i: (0, i, 0))]
        + [whole(shape) for shape in shapes],
        out_shape=[
            jax.ShapeDtypeStruct(shape, jnp.float32) for shape in [(3, count, capacity)] + shapes
        ],
        scratch_shapes=[
            pltpu.VMEM((6 * width_x * 8, COLUMNS), jnp.bfloat16),
            pltpu.VMEM((deposit_rows, COLUMNS), jnp.float32),
            pltpu.VMEM((BLOCKS, 3, SOURCES, capacity), jnp.float32),
            pltpu.VMEM((BLOCKS, 6 * reach, SOURCES, capacity), jnp.float32),
        ],
        compiler_params=pltpu.CompilerParams(vmem_limit_bytes=VMEM_BYTES),
        name="deposit",
    )(arrived, gas, sound)


def step_kernel(
    slab_ref, gas_ref, sound_ref, raw_ref, mine_left_ref, mine_right_ref,
    left_ref, right_ref, other_ref, next_ref,
):
    width_x, width_y, width_z = sound_ref.shape
    slab = slab_ref[0, 0]
    first_slab = slab == 0
    lane = lax.broadcasted_iota(jnp.int32, (width_y, width_z), 1)

    def along_y(f, shift):
        return pltpu.roll(f, (-shift) % width_y, 0)

    def along_z(f, other, shift):
        turned = pltpu.roll(f, (-shift) % width_z, 1)
        beyond = pltpu.roll(other, (-shift) % width_z, 1)
        if shift > 0:
            inside = lane < width_z - shift
            reached = first_slab
        else:
            inside = lane >= -shift
            reached = jnp.logical_not(first_slab)
        return jnp.where(inside, turned, jnp.where(reached, beyond, 0.0))

    def fourth(shifted):
        return (8.0 * (shifted(1) - shifted(-1)) - (shifted(2) - shifted(-2))) / 12.0

    def momentum(k, x):
        value = raw_ref[k, x]
        if x == 0:
            value = value + left_ref[4 + k]
        if x == width_x - 1:
            value = value + right_ref[4 + k]
        return value

    planes = [[momentum(k, x) for x in range(width_x)] for k in range(3)]
    first = {x: planes[0][x] for x in range(width_x)}
    first[-2] = left_ref[2]
    first[-1] = left_ref[3] + mine_left_ref[4]
    first[width_x] = right_ref[2] + mine_right_ref[4]
    first[width_x + 1] = right_ref[3]
    pressure = {x: sound_ref[x] * gas_ref[0, x] for x in range(width_x)}
    pressure[-2] = left_ref[0]
    pressure[-1] = left_ref[1]
    pressure[width_x] = right_ref[0]
    pressure[width_x + 1] = right_ref[1]
    for x in range(width_x):
        other = other_ref[x]
        if x == 0:
            other = other + left_ref[7]
        if x == width_x - 1:
            other = other + right_ref[7]
        other_p = other_ref[width_x + x]
        p = pressure[x]
        next_ref[0, x] = gas_ref[0, x] - courant * (
            fourth(lambda s: first[x + s])
            + fourth(lambda s: along_y(planes[1][x], s))
            + fourth(lambda s: along_z(planes[2][x], other, s))
        )
        next_ref[1, x] = planes[0][x] - courant * fourth(lambda s: pressure[x + s])
        next_ref[2, x] = planes[1][x] - courant * fourth(lambda s: along_y(p, s))
        next_ref[3, x] = planes[2][x] - courant * fourth(lambda s: along_z(p, other_p, s))


def gas_step(slab, gas, *rest):
    whole = pl.BlockSpec(memory_space=pltpu.VMEM)
    return pl.pallas_call(
        step_kernel,
        in_specs=[pl.BlockSpec(memory_space=pltpu.SMEM)] + [whole] * (1 + len(rest)),
        out_specs=whole,
        out_shape=jax.ShapeDtypeStruct(gas.shape, jnp.float32),
        compiler_params=pltpu.CompilerParams(vmem_limit_bytes=VMEM_BYTES),
        name="gas_step",
    )(slab, gas, *rest)


def per_device(
    gas_state, sound_speed, velocity, drag_rate, parcel_mass, cell_offset, target_owner,
    target_cell, live_counts,
):
    tiles = lax.axis_size("tile")
    slabs = lax.axis_size("slab")
    owner_count = tiles * slabs
    slot_count = target_cell.shape[-1]
    capacity = 3 * slot_count // (2 * owner_count)
    rows = slot_count // LANES
    width_x = gas_state.shape[1]
    to_right = [(t, (t + 1) % tiles) for t in range(tiles)]
    to_left = [(t, (t - 1) % tiles) for t in range(tiles)]
    swap = [(s, slabs - 1 - s) for s in range(slabs)]

    outbox = dispatch(
        live_counts,
        velocity.reshape(3, rows, LANES),
        drag_rate.reshape(rows, LANES),
        parcel_mass.reshape(rows, LANES),
        cell_offset.reshape(rows, LANES),
        target_owner.reshape(rows, LANES),
        target_cell.reshape(rows, LANES),
        owner_count,
        capacity,
    )
    arrived = lax.all_to_all(
        outbox.reshape(owner_count, 1, FIELDS * capacity), ("tile", "slab"),
        split_axis=0, concat_axis=0, tiled=True,
    ).reshape(outbox.shape)
    moved, raw, mine_right, mine_left, mine = deposit(
        arrived, gas_state, sound_speed, owner_count, capacity
    )
    other = lax.ppermute(mine, "slab", swap)
    left = lax.ppermute(
        jnp.concatenate([mine_right, other[2 * width_x + 1 :]]), "tile", to_right
    )
    right = lax.ppermute(
        jnp.concatenate([mine_left, other[2 * width_x : 2 * width_x + 1]]), "tile", to_left
    )
    slab = lax.axis_index("slab").astype(jnp.int32).reshape(1, 1)
    gas_next = gas_step(
        slab, gas_state, sound_speed, raw, mine_left, mine_right,
        left, right, other,
    )
    return gas_next, moved.reshape(3, 1, 1, owner_count, capacity)


def solution(mesh):
    return jax.shard_map(
        per_device,
        mesh=mesh,
        in_specs=(
            P(None, "tile", None, "slab"),
            P("tile", None, "slab"),
            P(None, "tile", "slab", None),
            P("tile", "slab", None),
            P("tile", "slab", None),
            P("tile", "slab", None),
            P("tile", "slab", None, None),
            P("tile", "slab", None),
            P("tile", "slab"),
        ),
        out_specs=(P(None, "tile", None, "slab"), P(None, "tile", "slab", None, None)),
        check_vma=False,
    )
```

```python
import functools

import jax
import jax.numpy as jnp
from jax import lax
from jax.experimental import pallas as pl
from jax.experimental.pallas import tpu as pltpu
from jax.sharding import PartitionSpec as P

courant = 0.4
LANES = 128
COLUMNS = 256
RES = 64
CHUNKS = 4
ROWS = 16
BLOCKS = 8
SOURCES = 8
FIELDS = 7
VMEM_BYTES = 40 * 1024 * 1024
COUNTED = jnp.float8_e4m3fn
NT = (((1,), (1,)), ((), ()))
NN = (((1,), (0,)), ((), ()))


def split2(x):
    hi = x.astype(jnp.bfloat16).astype(jnp.float32)
    return hi, x - hi


def dispatch_kernel(
    live_ref, vel_ref, rate_ref, mass_ref, off_ref, owner_ref, cell_ref, out_ref,
    acc, values, base, combined,
):
    owner_count = base.shape[0]
    windows = acc.shape[1]
    groups = acc.shape[2]
    pitch = out_ref.shape[0] // owner_count
    chunk = ROWS * LANES
    width = FIELDS * groups
    step = pl.program_id(0)
    f32, bf16 = jnp.float32, jnp.bfloat16

    @pl.when(step == 0)
    def _():
        acc[...] = jnp.zeros_like(acc)
        base[...] = jnp.zeros_like(base)

    def short_iota(rows):
        return lax.broadcasted_iota(jnp.int32, (rows, COLUMNS), 0).astype(f32).astype(bf16)

    def pair(x, t):
        return jnp.concatenate([x[2 * t : 2 * t + 1, :], x[2 * t + 1 : 2 * t + 2, :]], axis=1)

    def short_rows(row):
        return jnp.broadcast_to(row, (16, COLUMNS)).astype(bf16)

    one = jnp.ones((16, COLUMNS), bf16)
    zero = jnp.zeros((16, COLUMNS), bf16)

    def spread(row, rows):
        same = short_rows(row)
        numbers = short_iota(rows)
        return jnp.concatenate(
            [
                jnp.where(same == numbers[b * 16 : (b + 1) * 16], one, zero)
                for b in range(rows // 16)
            ],
            axis=0,
        )

    def multiply(group, picked, buffer):
        product = None
        numbers = short_iota(groups)
        for t in range(ROWS // 2):
            onehot = spread(pair(picked, t), COLUMNS)
            same = short_rows(pair(group, t))
            masks = [same == numbers[b * 16 : (b + 1) * 16] for b in range(groups // 16)]
            blocks = []
            for v in range(2 * FIELDS):
                value = short_rows(pair(values[buffer, v], t))
                for mask in masks:
                    blocks.append(jnp.where(mask, value, zero))
            part = lax.dot_general(
                jnp.concatenate(blocks, axis=0), onehot, NT, preferred_element_type=f32
            )
            product = part if product is None else product + part
        return product

    def add_product(product, start, number):
        product = product[:width] + product[width:]
        starts = start.astype(jnp.int32)
        lane = lax.broadcasted_iota(jnp.int32, (groups, LANES), 1)
        for k in range(COLUMNS // LANES):
            cols = slice(k * LANES, (k + 1) * LANES)
            even = starts[2 * k * groups : (2 * k + 1) * groups]
            odd = starts[(2 * k + 1) * groups : (2 * k + 2) * groups]
            first = jnp.where(lane < RES, even, odd) + number * RES
            window = (first + (((lane & (RES - 1)) - first) & (RES - 1))) >> 6
            for w in range(windows):
                here = window == w
                for v in range(FIELDS):
                    acc[v, w, :, cols] += jnp.where(
                        here, product[v * groups : (v + 1) * groups, cols], 0.0
                    )

    before = lax.broadcasted_iota(jnp.int32, (COLUMNS, COLUMNS), 0)
    after = lax.broadcasted_iota(jnp.int32, (COLUMNS, COLUMNS), 1)
    upper = jnp.where(before <= after, 1.0, 0.0).astype(COUNTED)
    owner_row = lax.broadcasted_iota(jnp.int32, (owner_count, LANES), 0)

    def rank_slots(h):
        part = slice(h * ROWS, (h + 1) * ROWS)
        slot = (
            (CHUNKS * step + h) * chunk
            + lax.broadcasted_iota(jnp.int32, (ROWS, LANES), 0) * LANES
            + lax.broadcasted_iota(jnp.int32, (ROWS, LANES), 1)
        )
        alive = slot < live_ref[0, 0]
        dest = jnp.where(alive, owner_ref[part], owner_count)
        destf = dest.astype(f32)
        start = base[...]
        running = start * float(chunk)
        owners = jnp.concatenate(
            [spread(pair(destf, t), owner_count) for t in range(ROWS // 2)], axis=0
        )
        priors = lax.dot_general(owners.astype(COUNTED), upper, NN, preferred_element_type=f32)
        for t in range(ROWS // 2):
            prior = priors[t * owner_count : (t + 1) * owner_count]
            for half in range(2):
                j = 2 * t + half
                total = prior[:, half * LANES : (half + 1) * LANES] + running
                combined[j : j + 1, :] = jnp.sum(
                    jnp.where(dest[j : j + 1, :] == owner_row, total, 0.0), axis=0, keepdims=True
                )
            running = running + jnp.broadcast_to(prior[:, COLUMNS - 1 :], (owner_count, LANES))
        tally = running - start * float(chunk)
        base[...] = start + tally
        both = combined[...].astype(jnp.int32) - 1
        local_rank = both & (chunk - 1)
        rank = local_rank + (both >> 11)
        column = (dest // groups) * RES + (rank & (RES - 1))
        turn = jnp.where(alive, local_rank >> 6, -1)
        fields = [
            vel_ref[0, part], vel_ref[1, part], vel_ref[2, part], rate_ref[part], mass_ref[part],
            off_ref[part], cell_ref[part].astype(f32),
        ]
        for v, field in enumerate(fields):
            hi, lo = split2(field)
            values[h, v] = hi
            values[h, v + FIELDS] = lo
        group = (dest & (groups - 1)).astype(f32)
        return tally, turn, column, group, start

    def one_pass(h, state, number):
        _, turn, column, group, start = state
        picked = jnp.where(turn == number, column, -1).astype(f32)
        add_product(multiply(group, picked, h), start, number)

    states = [rank_slots(h) for h in range(CHUNKS)]
    for h in range(CHUNKS):
        one_pass(h, states[h], 0)

    def passes(tally):
        return (jnp.max(tally).astype(jnp.int32) + RES - 1) >> 6

    @pl.when(passes(functools.reduce(jnp.maximum, [state[0] for state in states])) > 1)
    def _():
        for h in range(CHUNKS):
            def body(number, carry):
                one_pass(h, states[h], number)
                return carry

            lax.fori_loop(1, passes(states[h][0]), body, 0)

    @pl.when(step == pl.num_programs(0) - 1)
    def _():
        low = lax.broadcasted_iota(jnp.int32, (8, LANES), 1) < RES
        for v in range(FIELDS):
            for k in range(COLUMNS // LANES):
                cols = slice(k * LANES, (k + 1) * LANES)
                for m in range(windows // 2):
                    for part in range(groups // 8):
                        rows = slice(part * 8, (part + 1) * 8)
                        near = acc[v, 2 * m, rows, cols]
                        far = acc[v, 2 * m + 1, rows, cols]
                        place = v * (windows // 2) + m
                        even = (2 * k * groups + part * 8) * pitch + place
                        odd = ((2 * k + 1) * groups + part * 8) * pitch + place
                        out_ref[pl.ds(even, 8, stride=pitch), :] = jnp.where(
                            low, near, pltpu.roll(far, RES, 1)
                        )
                        out_ref[pl.ds(odd, 8, stride=pitch), :] = jnp.where(
                            low, pltpu.roll(near, RES, 1), far
                        )


def dispatch(live, vel, rate, mass, off, owner, cell, owner_count, capacity):
    rows = rate.shape[0]
    groups = owner_count * RES // COLUMNS
    pitch = FIELDS * capacity // LANES
    plain = pl.BlockSpec((CHUNKS * ROWS, LANES), lambda i: (i, 0))
    return pl.pallas_call(
        dispatch_kernel,
        grid=(rows // (CHUNKS * ROWS),),
        in_specs=[
            pl.BlockSpec(memory_space=pltpu.SMEM),
            pl.BlockSpec((3, CHUNKS * ROWS, LANES), lambda i: (0, i, 0)),
            plain, plain, plain, plain, plain,
        ],
        out_specs=pl.BlockSpec((owner_count * pitch, LANES), lambda i: (0, 0)),
        out_shape=jax.ShapeDtypeStruct((owner_count * pitch, LANES), jnp.float32),
        scratch_shapes=[
            pltpu.VMEM((FIELDS, capacity // RES, groups, COLUMNS), jnp.float32),
            pltpu.VMEM((CHUNKS, 2 * FIELDS, ROWS, LANES), jnp.float32),
            pltpu.VMEM((owner_count, LANES), jnp.float32),
            pltpu.VMEM((ROWS, LANES), jnp.float32),
        ],
        compiler_params=pltpu.CompilerParams(vmem_limit_bytes=60 * 1024 * 1024),
        name="dispatch",
    )(live, vel, rate, mass, off, owner, cell)


def deposit_kernel(
    arrived_ref, gas_ref, sound_ref,
    moved_ref, raw_ref, to_right_ref, to_left_ref, to_other_ref,
    table, total, speeds, pieces,
):
    capacity = moved_ref.shape[2]
    width_x = gas_ref.shape[1]
    reach = width_x + 2
    strips = 8
    rows = width_x * strips
    half = 3 * reach * strips
    pitch = arrived_ref.shape[0] // (BLOCKS * SOURCES)
    parts = capacity // LANES
    units = [(s, m) for m in range(parts) for s in range(SOURCES)]
    f32, bf16 = jnp.float32, jnp.bfloat16
    step = pl.program_id(0)

    @pl.when(step == 0)
    def _():
        total[...] = jnp.zeros_like(total)
        for v in range(3):
            for x in range(0, width_x, 2):
                for h in range(2):
                    two = [gas_ref[1 + v, x + i, h * 8 : (h + 1) * 8, :] for i in range(2)]
                    hi, lo = split2(jnp.concatenate(two, axis=0))
                    at = v * rows + x * strips
                    cols = slice(h * LANES, (h + 1) * LANES)
                    table[at : at + 16, cols] = hi.astype(bf16)
                    table[3 * rows + at : 3 * rows + at + 16, cols] = lo.astype(bf16)

    one = jnp.ones((16, COLUMNS), bf16)
    zero = jnp.zeros((16, COLUMNS), bf16)
    number = lax.broadcasted_iota(jnp.int32, (16, COLUMNS), 0)
    numbers = [(number + 16 * b).astype(f32).astype(bf16) for b in range(COLUMNS // 16)]
    strip_number = (number & (strips - 1)).astype(f32).astype(bf16)
    row_row = lax.broadcasted_iota(jnp.int32, (rows, LANES), 0)

    def cut(x, unit):
        s, m = unit
        return x[s : s + 1, m * LANES : (m + 1) * LANES]

    def pair(x, u):
        return jnp.concatenate([cut(x, units[u]), cut(x, units[u + 1])], axis=1)

    def short_rows(row):
        return jnp.broadcast_to(row, (16, COLUMNS)).astype(bf16)

    def spread(column, u):
        same = short_rows(pair(column, u))
        return jnp.concatenate([jnp.where(same == n, one, zero) for n in numbers], axis=0)

    def field(h, v):
        first = h * SOURCES * pitch + v * parts
        return jnp.concatenate(
            [arrived_ref[pl.ds(first + m, SOURCES, stride=pitch), :] for m in range(parts)], axis=1
        )

    def look_up(h):
        cell = field(h, 6).astype(jnp.int32)
        column = ((cell & (LANES - 1)) + ((cell >> 10) & 1) * LANES).astype(f32)
        strip = (cell >> 7) & (strips - 1)
        row = (cell >> 11) * strips + strip
        for u in range(0, len(units), 2):
            found = lax.dot_general(
                table[...], spread(column, u), NN, preferred_element_type=f32
            )
            found = found[: 3 * rows] + found[3 * rows :]
            for i in range(2):
                s, m = units[u + i]
                mask = cut(row, units[u + i]) == row_row
                for v in range(3):
                    mine = found[v * rows : (v + 1) * rows, i * LANES : (i + 1) * LANES]
                    speeds[h, v, s : s + 1, m * LANES : (m + 1) * LANES] = jnp.sum(
                        jnp.where(mask, mine, 0.0), axis=0, keepdims=True
                    )
        return cell, column, strip.astype(f32)

    def relax(h, cell):
        part = slice(h * SOURCES, (h + 1) * SOURCES)
        plane = cell >> 11
        rate = field(h, 3)
        mass = field(h, 4)
        shift = field(h, 5)
        occupied = mass > 0.0
        low_weight = 0.5 * (0.5 - shift) ** 2
        mid_weight = 0.75 - shift**2
        high_weight = 0.5 * (0.5 + shift) ** 2
        weights = []
        for x in range(reach):
            rest = jnp.where(plane == x - 2, high_weight, 0.0)
            rest = jnp.where(plane == x - 1, mid_weight, rest)
            weights.append(jnp.where(plane == x, low_weight, rest))
        for v in range(3):
            speed = field(h, v)
            slip = speed - speeds[h, v]
            moved_ref[v, part] = jnp.where(occupied, speed - rate * slip, 0.0)
            kick = mass * rate * slip
            for x in range(reach):
                hi, lo = split2(kick * weights[x])
                pieces[h, v * reach + x] = hi
                pieces[h, (3 + v) * reach + x] = lo

    def gather_up(h, column, strip):
        product = None
        for u in range(0, len(units), 2):
            mask = short_rows(pair(strip, u)) == strip_number
            blocks = []
            for p in range(3 * reach):
                both = [
                    jnp.broadcast_to(pair(pieces[h, 2 * p + i], u), (strips, COLUMNS))
                    for i in range(2)
                ]
                blocks.append(jnp.where(mask, jnp.concatenate(both, axis=0).astype(bf16), zero))
            part = lax.dot_general(
                jnp.concatenate(blocks, axis=0), spread(column, u), NT, preferred_element_type=f32
            )
            product = part if product is None else product + part
        total[...] = total[...] + (product[:half] + product[half:])

    found = [look_up(h) for h in range(BLOCKS)]
    for h in range(BLOCKS):
        relax(h, found[h][0])
    for h in range(BLOCKS):
        gather_up(h, *found[h][1:])

    @pl.when(step == pl.num_programs(0) - 1)
    def _():
        def added(v, x):
            at = (v * reach + x) * strips
            return jnp.concatenate(
                [total[at : at + strips, h * LANES : (h + 1) * LANES] for h in range(2)], axis=0
            )

        for v in range(3):
            to_left_ref[4 + v] = added(v, 0)
            to_right_ref[4 + v] = added(v, width_x + 1)
            for x in range(width_x):
                raw_ref[v, x] = gas_ref[1 + v, x] + added(v, x + 1)
        to_other_ref[2 * width_x] = added(2, 0)
        to_other_ref[2 * width_x + 1] = added(2, width_x + 1)
        for x in range(width_x):
            pressure = sound_ref[x] * gas_ref[0, x]
            to_other_ref[x] = raw_ref[2, x]
            to_other_ref[width_x + x] = pressure
            if x < 2:
                to_left_ref[x] = pressure
                to_left_ref[2 + x] = raw_ref[0, x]
            if x >= width_x - 2:
                to_right_ref[x - width_x + 2] = pressure
                to_right_ref[x - width_x + 4] = raw_ref[0, x]


def deposit(arrived, gas, sound, count, capacity):
    pitch = arrived.shape[0] // count
    width_x, width_y, width_z = gas.shape[1:]
    reach = width_x + 2
    deposit_rows = 3 * reach * 8
    plane = (width_y, width_z)
    shapes = [(3, width_x) + plane, (7,) + plane, (7,) + plane, (2 * width_x + 2,) + plane]

    def whole(shape):
        return pl.BlockSpec(shape, lambda i: (0,) * len(shape))

    return pl.pallas_call(
        deposit_kernel,
        grid=(count // (BLOCKS * SOURCES),),
        in_specs=[
            pl.BlockSpec((BLOCKS * SOURCES * pitch, LANES), lambda i: (i, 0)),
            whole(gas.shape),
            whole(sound.shape),
        ],
        out_specs=[pl.BlockSpec((3, BLOCKS * SOURCES, capacity), lambda i: (0, i, 0))]
        + [whole(shape) for shape in shapes],
        out_shape=[
            jax.ShapeDtypeStruct(shape, jnp.float32) for shape in [(3, count, capacity)] + shapes
        ],
        scratch_shapes=[
            pltpu.VMEM((6 * width_x * 8, COLUMNS), jnp.bfloat16),
            pltpu.VMEM((deposit_rows, COLUMNS), jnp.float32),
            pltpu.VMEM((BLOCKS, 3, SOURCES, capacity), jnp.float32),
            pltpu.VMEM((BLOCKS, 6 * reach, SOURCES, capacity), jnp.float32),
        ],
        compiler_params=pltpu.CompilerParams(vmem_limit_bytes=VMEM_BYTES),
        name="deposit",
    )(arrived, gas, sound)


def step_kernel(
    slab_ref, gas_ref, sound_ref, raw_ref, mine_left_ref, mine_right_ref,
    left_ref, right_ref, other_ref, next_ref,
):
    width_x, width_y, width_z = sound_ref.shape
    slab = slab_ref[0, 0]
    first_slab = slab == 0
    lane = lax.broadcasted_iota(jnp.int32, (width_y, width_z), 1)

    def along_y(f, shift):
        return pltpu.roll(f, (-shift) % width_y, 0)

    def along_z(f, other, shift):
        turned = pltpu.roll(f, (-shift) % width_z, 1)
        beyond = pltpu.roll(other, (-shift) % width_z, 1)
        if shift > 0:
            inside = lane < width_z - shift
            reached = first_slab
        else:
            inside = lane >= -shift
            reached = jnp.logical_not(first_slab)
        return jnp.where(inside, turned, jnp.where(reached, beyond, 0.0))

    def fourth(shifted):
        return (8.0 * (shifted(1) - shifted(-1)) - (shifted(2) - shifted(-2))) / 12.0

    def momentum(k, x):
        value = raw_ref[k, x]
        if x == 0:
            value = value + left_ref[4 + k]
        if x == width_x - 1:
            value = value + right_ref[4 + k]
        return value

    planes = [[momentum(k, x) for x in range(width_x)] for k in range(3)]
    first = {x: planes[0][x] for x in range(width_x)}
    first[-2] = left_ref[2]
    first[-1] = left_ref[3] + mine_left_ref[4]
    first[width_x] = right_ref[2] + mine_right_ref[4]
    first[width_x + 1] = right_ref[3]
    pressure = {x: sound_ref[x] * gas_ref[0, x] for x in range(width_x)}
    pressure[-2] = left_ref[0]
    pressure[-1] = left_ref[1]
    pressure[width_x] = right_ref[0]
    pressure[width_x + 1] = right_ref[1]
    for x in range(width_x):
        other = other_ref[x]
        if x == 0:
            other = other + left_ref[7]
        if x == width_x - 1:
            other = other + right_ref[7]
        other_p = other_ref[width_x + x]
        p = pressure[x]
        next_ref[0, x] = gas_ref[0, x] - courant * (
            fourth(lambda s: first[x + s])
            + fourth(lambda s: along_y(planes[1][x], s))
            + fourth(lambda s: along_z(planes[2][x], other, s))
        )
        next_ref[1, x] = planes[0][x] - courant * fourth(lambda s: pressure[x + s])
        next_ref[2, x] = planes[1][x] - courant * fourth(lambda s: along_y(p, s))
        next_ref[3, x] = planes[2][x] - courant * fourth(lambda s: along_z(p, other_p, s))


def gas_step(slab, gas, *rest):
    whole = pl.BlockSpec(memory_space=pltpu.VMEM)
    return pl.pallas_call(
        step_kernel,
        in_specs=[pl.BlockSpec(memory_space=pltpu.SMEM)] + [whole] * (1 + len(rest)),
        out_specs=whole,
        out_shape=jax.ShapeDtypeStruct(gas.shape, jnp.float32),
        compiler_params=pltpu.CompilerParams(vmem_limit_bytes=VMEM_BYTES),
        name="gas_step",
    )(slab, gas, *rest)


def per_device(
    gas_state, sound_speed, velocity, drag_rate, parcel_mass, cell_offset, target_owner,
    target_cell, live_counts,
):
    tiles = lax.axis_size("tile")
    slabs = lax.axis_size("slab")
    owner_count = tiles * slabs
    slot_count = target_cell.shape[-1]
    capacity = 3 * slot_count // (2 * owner_count)
    rows = slot_count // LANES
    width_x = gas_state.shape[1]
    to_right = [(t, (t + 1) % tiles) for t in range(tiles)]
    to_left = [(t, (t - 1) % tiles) for t in range(tiles)]
    swap = [(s, slabs - 1 - s) for s in range(slabs)]

    outbox = dispatch(
        live_counts,
        velocity.reshape(3, rows, LANES),
        drag_rate.reshape(rows, LANES),
        parcel_mass.reshape(rows, LANES),
        cell_offset.reshape(rows, LANES),
        target_owner.reshape(rows, LANES),
        target_cell.reshape(rows, LANES),
        owner_count,
        capacity,
    )
    arrived = lax.all_to_all(
        outbox.reshape(owner_count, 1, FIELDS * capacity), ("tile", "slab"),
        split_axis=0, concat_axis=0, tiled=True,
    ).reshape(outbox.shape)
    moved, raw, mine_right, mine_left, mine = deposit(
        arrived, gas_state, sound_speed, owner_count, capacity
    )
    other = lax.ppermute(mine, "slab", swap)
    left = lax.ppermute(
        jnp.concatenate([mine_right, other[2 * width_x + 1 :]]), "tile", to_right
    )
    right = lax.ppermute(
        jnp.concatenate([mine_left, other[2 * width_x : 2 * width_x + 1]]), "tile", to_left
    )
    slab = lax.axis_index("slab").astype(jnp.int32).reshape(1, 1)
    gas_next = gas_step(
        slab, gas_state, sound_speed, raw, mine_left, mine_right,
        left, right, other,
    )
    return gas_next, moved.reshape(3, 1, 1, owner_count, capacity)


def solution(mesh):
    return jax.shard_map(
        per_device,
        mesh=mesh,
        in_specs=(
            P(None, "tile", None, "slab"),
            P("tile", None, "slab"),
            P(None, "tile", "slab", None),
            P("tile", "slab", None),
            P("tile", "slab", None),
            P("tile", "slab", None),
            P("tile", "slab", None, None),
            P("tile", "slab", None),
            P("tile", "slab"),
        ),
        out_specs=(P(None, "tile", None, "slab"), P(None, "tile", "slab", None, None)),
        check_vma=False,
    )
```
